256 devices in a mesh: fsdp: 32 (over x, z_hi, core), tp: 8 (over z_lo, y).
Axes of the slice: x: 4, y: 4, z: 8 (z_hi: 4, z_lo: 2; z = z_hi * 2 + z_lo), core: 2. Of those that a mesh axis runs over, the one named last changes fastest.
Arguments:
- master: float32 [8192, 2048], P('fsdp', 'tp'), may hold values from -0.0625 to 0.0625
- grad: bfloat16 [8192, 2048], P('fsdp', 'tp'), may hold values from -6 to 6
- moment: float32 [8192, 2048], P('fsdp', 'tp'), may hold values from -4 to 4
- variance: float32 [8192, 2048], P('fsdp', 'tp'), may hold values from 0.01 to 1
- q_left: bfloat16 [8192, 8192], P(None, 'fsdp'), may hold values from -0.0625 to 0.0625
- q_right: bfloat16 [2048, 2048], P(None, 'tp'), may hold values from -0.125 to 0.125
- embed: bfloat16 [76032, 8192], P('tp', 'fsdp')
- gain: float32 [8192], replicated, may hold values from 0.5 to 1.5
- token_ids: int32 [128, 4], replicated, may hold values from 0 to 76031
- queries: bfloat16 [128, 4, 8192], P('fsdp', None, 'tp')
- k_cache: bfloat16 [128, 8, 512, 128], P('fsdp', 'tp')
- v_cache: bfloat16 [128, 8, 512, 128], P('fsdp', 'tp'), may hold values from -6 to 6
- cache_len: int32 [128], P('fsdp'), may hold values from 1 to 512, as said below
Outputs:
- update: float32 [8192, 2048], P('fsdp', 'tp')
- moment_new: float32 [8192, 2048], P('fsdp', 'tp')
- variance_new: float32 [8192, 2048], P('fsdp', 'tp')
- attended: float32 [128, 4, 8192], P('fsdp', None, 'tp')
The draws below stay inside these ranges and needn't reach their ends.
Inputs may be any that keep to these rules, and one draw needn't show every extreme that they name: `cache_len`: at least one sequence has exactly 512 cached positions.
All inputs are finite; a program needn't handle non-finite values.
Results may differ from the reference program's by a relative error of at most 0.022.
Values may be sent and summed in bfloat16 or wider, within the bound.
No kernel may reach another device: no remote copies, remote signals or barrier semaphores. Data moves between devices by JAX's collectives and lax.ppermute only.
A program may use at most 64 MiB of HBM per device.

```python
import math
import jax
import jax.numpy as jnp
import numpy as np
from jax import lax

D = 8192
QH = 64
KVH = 8
HD = 128
V_SL = 76032
STEPS = 4
CACHE = 512
C = 2048
SEQ_TOT = 128


def shared_keys(key):
    return jax.random.normal(key, (SEQ_TOT, KVH, CACHE, HD), jnp.float32)


def draw_k_cache(key, part):
    base = shared_keys(key)
    return base.astype(jnp.bfloat16)


def draw_queries(key, part):
    key = jax.random.fold_in(key, 12)
    key_one = jax.random.fold_in(key, 0)
    values = jax.random.normal(key_one, (SEQ_TOT, STEPS, QH * HD), jnp.float32)
    return values.astype(jnp.bfloat16)


def draw_cache_len(key, part):
    key = jax.random.fold_in(key, 13)
    lengths = jax.random.randint(key, (SEQ_TOT,), 1, CACHE + 1, jnp.int32)
    return lengths.at[0].set(CACHE)


def draw_embed(key, part):
    key = jax.random.fold_in(key, 14)
    key_one, key_two = jax.random.split(key, 2)
    col_scale = jnp.exp(jax.random.uniform(key_two, (1, D), jnp.float32, math.log(0.3), math.log(3.0)))
    values = jax.random.normal(key_one, (V_SL, D), jnp.float32)
    return (values * col_scale).astype(jnp.bfloat16)


def with_ends(drawn, rng, least, high):
    longest = drawn.shape.index(max(drawn.shape))
    spots = []
    for shift in (0, 1):
        where = [jax.random.randint(jax.random.fold_in(rng, axis), (), 0, length) for axis, length in enumerate(drawn.shape)]
        where[longest] = (where[longest] + shift) % drawn.shape[longest]
        spots.append(tuple(where))
    return drawn.at[spots[0]].set(least).at[spots[1]].set(high)


def shard_levels(stream_key, dims, pieces, least, high):
    level, own = 1.0, jax.random.fold_in(stream_key, 6)
    for axis_at, shards_of in pieces:
        draws = jnp.exp(jax.random.uniform(jax.random.fold_in(own, axis_at), (shards_of,), jnp.float32, least / len(pieces), high / len(pieces)))
        level = level * jnp.repeat(draws, dims[axis_at] // shards_of).reshape([-1 if axis == axis_at else 1 for axis in range(len(dims))])
    return level


def wide_ids(own_key, dims, number_of, lean):
    portions = [min(1 << octave, number_of + 1 - (1 << octave)) * (1 << 20) // math.isqrt((1 << octave) ** lean) + 1 for octave in range((number_of + 1).bit_length()) if 1 << octave <= number_of]
    spread = 1 + sum(portions) // (1 << 30)
    listing = np.cumsum(np.array([max(1, weight // spread) for weight in portions]))
    pick = jax.random.randint(jax.random.fold_in(own_key, 1), dims, 0, int(listing[len(portions) - 1]))
    start = jnp.left_shift(1, jnp.searchsorted(jnp.asarray(listing, jnp.int32), pick, side="right").astype(jnp.int32))
    rank = start - 1 + jax.random.randint(jax.random.fold_in(own_key, 4), dims, 0, 1 << 30) % jnp.minimum(start, number_of + 1 - start)
    return jax.random.permutation(jax.random.fold_in(own_key, 2), number_of)[rank].astype(jnp.int32)


def centred(rng, dims, scale, most, shards=(), kind=jnp.bfloat16):
    array = scale * jax.random.normal(rng, dims, jnp.float32)
    if shards:
        array = array * shard_levels(rng, dims, shards, -0.22, 0.18)
    return jnp.clip(array, -most, most).astype(kind)


def setup_inputs(seed: int = 0) -> dict:
    key_list = jax.random.split(jax.random.key(seed), 14)
    return {
        "master": centred(key_list[0], (D, C), D ** -0.5, 0.0625, ((0, 32), (1, 8)), jnp.float32),
        "grad": centred(key_list[1], (D, C), 1.0, 6.0, ((0, 32), (1, 8))),
        "moment": centred(key_list[2], (D, C), 0.3, 4.0, ((0, 32), (1, 8)), jnp.float32),
        "variance": jnp.clip(jnp.exp(math.log(1.0) - 4.6051702 * jax.random.uniform(key_list[3], (D, C), jnp.float32) ** shard_levels(key_list[3], (D, C), ((0, 32), (1, 8)), -0.2, 0.2)), 0.01, 1.0),
        "q_left": centred(key_list[4], (D, D), D ** -0.5, 0.0625, ((1, 32),)),
        "q_right": centred(key_list[5], (C, C), C ** -0.5, 0.125, ((1, 8),)),
        "embed": draw_embed(jax.random.fold_in(key_list[13], 71), 0),
        "gain": jnp.clip(1.0 + 0.1 * jax.random.normal(key_list[7], (D,), jnp.float32), 0.5, 1.5),
        "token_ids": with_ends(wide_ids(key_list[8], (SEQ_TOT, STEPS), V_SL, 2), jax.random.fold_in(key_list[8], 3), 0, V_SL - 1).astype(jnp.int32),
        "queries": draw_queries(jax.random.fold_in(key_list[13], 71), 0),
        "k_cache": draw_k_cache(jax.random.fold_in(key_list[13], 71), 0),
        "v_cache": centred(key_list[11], (SEQ_TOT, KVH, CACHE, HD), 1.0, 6.0, ((0, 32), (1, 8))),
        "cache_len": draw_cache_len(jax.random.fold_in(key_list[13], 71), 0),
    }


beta_one = 0.9
beta_two = 0.95
adam_eps = 1e-08
learn_rate = 0.003
adam_step = 20
norm_eps = 1e-06
rope_base = 1000000.0

def rotary(vectors, positions):
    head_dim = vectors.shape[-1]
    half_dim = head_dim // 2
    inverse = rope_base ** (-(jnp.arange(half_dim, dtype=jnp.float32) * 2.0 / head_dim))
    angles = positions[..., None].astype(jnp.float32) * inverse
    cosine = jnp.cos(angles)
    sine_part = jnp.sin(angles)
    first_half = vectors[..., :half_dim]
    second_half = vectors[..., half_dim:]
    return jnp.concatenate([first_half * cosine - second_half * sine_part, second_half * cosine + first_half * sine_part], -1)

def attend(queries, k_cache, v_cache, k_new, v_new, cache_len):
    seqs = queries.shape[0]
    steps = queries.shape[1]
    heads_kv = k_cache.shape[1]
    head_dim = k_cache.shape[3]
    scaling = float(head_dim) ** (-0.5)
    query_f = queries.reshape(seqs, steps, heads_kv, -1, head_dim).astype(jnp.float32)
    score_old = jnp.einsum('stkgd,skcd->sktgc', query_f, k_cache.astype(jnp.float32)) * scaling
    score_new = jnp.einsum('stkgd,sjkd->sktgj', query_f, k_new.astype(jnp.float32)) * scaling
    old_mask = (jnp.arange(k_cache.shape[2], dtype=jnp.int32)[None, :] < cache_len[:, None])[:, None, None, None, :]
    step_ids = jnp.arange(steps, dtype=jnp.int32)
    new_mask = (step_ids[None, :] <= step_ids[:, None])[None, None, :, None, :]
    score_old = jnp.where(old_mask, score_old, -1e+30)
    score_new = jnp.where(new_mask, score_new, -1e+30)
    row_max = jnp.maximum(lax.optimization_barrier(jnp.max(score_old, -1)), lax.optimization_barrier(jnp.max(score_new, -1)))[..., None]
    exp_old = jnp.where(old_mask, jnp.exp(score_old - row_max), 0.0)
    exp_new = jnp.where(new_mask, jnp.exp(score_new - row_max), 0.0)
    totals = lax.optimization_barrier(jnp.sum(exp_old, -1, keepdims=True)) + lax.optimization_barrier(jnp.sum(exp_new, -1, keepdims=True))
    prob_old = (exp_old / totals).astype(jnp.bfloat16)
    prob_new = (exp_new / totals).astype(jnp.bfloat16)
    output = jnp.einsum('sktgc,skcd->stkgd', prob_old.astype(jnp.float32), v_cache.astype(jnp.float32))
    output = output + jnp.einsum('sktgj,sjkd->stkgd', prob_new.astype(jnp.float32), v_new.astype(jnp.float32))
    return output.reshape(seqs, steps, -1)

def reference(master, grad, moment, variance, q_left, q_right, embed, gain, token_ids, queries, k_cache, v_cache, cache_len):
    moment_new = beta_one * moment + (1.0 - beta_one) * grad.astype(jnp.float32)
    moment_low = moment_new.astype(jnp.bfloat16)
    left_g = jnp.dot(q_left.T, grad, preferred_element_type=jnp.float32).astype(jnp.bfloat16)
    left_m = jnp.dot(q_left.T, moment_low, preferred_element_type=jnp.float32).astype(jnp.bfloat16)
    rot_g = jnp.dot(left_g, q_right, preferred_element_type=jnp.float32)
    rot_m = jnp.dot(left_m, q_right, preferred_element_type=jnp.float32)
    variance_new = beta_two * variance + (1.0 - beta_two) * rot_g * rot_g
    corr_one = 1.0 - beta_one ** adam_step
    corr_two = 1.0 - beta_two ** adam_step
    direction = (rot_m / corr_one / (jnp.sqrt(variance_new / corr_two) + adam_eps)).astype(jnp.bfloat16)
    back = jnp.dot(direction, q_right.T, preferred_element_type=jnp.float32).astype(jnp.bfloat16)
    update = jnp.dot(q_left, back, preferred_element_type=jnp.float32)
    weight = (master - learn_rate * update).astype(jnp.bfloat16)
    rows = jnp.take(embed, token_ids.reshape(-1), axis=0)
    features = rows.astype(jnp.float32)
    mean_square = lax.optimization_barrier(jnp.mean(features * features, -1, keepdims=True))
    normed = (features * lax.rsqrt(mean_square + norm_eps) * gain).astype(jnp.bfloat16)
    key_value = jnp.dot(normed, weight, preferred_element_type=jnp.float32)
    key_value = key_value.reshape(SEQ_TOT, STEPS, KVH, 2, HD)
    positions = cache_len[:, None] + jnp.arange(STEPS, dtype=jnp.int32)[None, :]
    k_new = rotary(key_value[:, :, :, 0], positions[:, :, None]).astype(jnp.bfloat16)
    v_new = key_value[:, :, :, 1].astype(jnp.bfloat16)
    attended = attend(queries, k_cache, v_cache, k_new, v_new, cache_len)
    return (update, moment_new, variance_new, attended)
```

```python
import jax
import jax.numpy as jnp
from jax import lax
from jax.sharding import Mesh, PartitionSpec as P

beta_one = 0.9
beta_two = 0.95
adam_eps = 1e-08
learn_rate = 0.003
adam_step = 20
norm_eps = 1e-06
rope_base = 1000000.0

AXES = ("x", "zh", "c", "zl", "y")
SIZES = {"x": 4, "zh": 4, "c": 2, "zl": 2, "y": 4}
f32 = jnp.float32
bf16 = jnp.bfloat16


def rotary(vectors, positions):
    head_dim = vectors.shape[-1]
    half_dim = head_dim // 2
    inverse = rope_base ** (-(jnp.arange(half_dim, dtype=f32) * 2.0 / head_dim))
    angles = positions[..., None].astype(f32) * inverse
    cosine = jnp.cos(angles)
    sine_part = jnp.sin(angles)
    first_half = vectors[..., :half_dim]
    second_half = vectors[..., half_dim:]
    return jnp.concatenate(
        [
            first_half * cosine - second_half * sine_part,
            second_half * cosine + first_half * sine_part,
        ],
        -1,
    )


def shift(array, axis, by):
    size = SIZES[axis]
    return lax.ppermute(array, axis, [(i, (i + by) % size) for i in range(size)])


def gather_pieces(array, axis):
    return [array] + [shift(array, axis, k) for k in range(1, SIZES[axis])]


def scatter_pieces(array, axis):
    return [array[0]] + [shift(array[k], axis, -k) for k in range(1, SIZES[axis])]


def swap(array):
    return shift(array, "c", 1)


def by_core(core, own, other, axis):
    return jnp.where(
        core == 0,
        jnp.concatenate([own, other], axis),
        jnp.concatenate([other, own], axis),
    )


def pick(array, index, axis):
    return lax.dynamic_index_in_dim(array, index, axis, keepdims=False)


def dot(left, right, left_dim, right_dim):
    return lax.dot_general(
        left, right, (((left_dim,), (right_dim,)), ((), ())), preferred_element_type=f32
    )


def shards(
    master,
    grad,
    moment,
    variance,
    q_left,
    q_right,
    embed,
    gain,
    token_ids,
    queries,
    k_cache,
    v_cache,
    cache_len,
):
    at = {name: lax.axis_index(name) for name in AXES}
    core = at["c"]
    rows, cols = grad.shape
    half = cols // 2
    feats = q_left.shape[0]
    chip_rows = 2 * rows
    n_x, n_z, n_y, n_l = SIZES["x"], SIZES["zh"], SIZES["y"], SIZES["zl"]

    def before_xz(i, j):
        return ((at["x"] - i) % n_x) * n_z + (at["zh"] - j) % n_z

    def before_ly(i, j):
        return ((at["zl"] - i) % n_l) * n_y + (at["y"] - j) % n_y

    xz_order = [before_xz(i, j) for i in range(n_x) for j in range(n_z)]
    ly_order = [before_ly(i, j) for i in range(n_l) for j in range(n_y)]

    def reorder(array, order):
        return jnp.stack([pick(array, index, 0) for index in order], 0)

    def chip_halves(block):
        parts = block.reshape(rows, 2, half)
        return by_core(core, pick(parts, core, 1), swap(pick(parts, 1 - core, 1)), 0)

    def chip_gather(block):
        block = jnp.concatenate(gather_pieces(block, "zh"), 0)
        return gather_pieces(block, "x")

    grad_pieces = chip_gather(chip_halves(grad))
    moment_new = beta_one * moment + (1.0 - beta_one) * grad.astype(f32)
    moment_pieces = chip_gather(chip_halves(moment_new.astype(bf16)))

    basis_own = reorder(q_left.reshape(n_x * n_z, chip_rows, rows), xz_order).reshape(
        n_x, n_z * chip_rows, rows
    )
    basis_other = swap(basis_own)
    right_blocks = q_right.reshape(n_l * n_y, cols, cols)
    right_in = reorder(right_blocks, ly_order).reshape(-1, cols)
    right_out = lax.all_to_all(right_blocks, ("zl", "y"), 0, 0, tiled=True)
    right_out = reorder(right_out, ly_order)

    flat_ids = token_ids.reshape(-1)
    n_tok = flat_ids.shape[0]
    vocab_rows = embed.shape[0]
    local_ids = flat_ids - (at["zl"] * n_y + at["y"]) * vocab_rows
    inside = (local_ids >= 0) & (local_ids < vocab_rows)
    picked = jnp.take(embed, jnp.clip(local_ids, 0, vocab_rows - 1), axis=0)
    picked = jnp.where(inside[:, None], picked, jnp.zeros_like(picked))
    block = n_tok // (n_x * n_z)
    picked = picked.reshape(n_y, n_l, 2, block, rows)
    picked = by_core(core, pick(picked, core, 2), swap(pick(picked, 1 - core, 2)), -1)
    picked = jnp.swapaxes(picked, 0, 1).reshape(n_l * n_y, block, chip_rows)
    arrived = lax.all_to_all(picked, ("zl", "y"), 0, 0, tiled=True)
    tokens_here = jnp.sum(arrived.astype(f32), 0).astype(bf16)
    features = jnp.concatenate(gather_pieces(tokens_here, "zh"), 1)
    features = jnp.concatenate(gather_pieces(features, "x"), 1).astype(f32)
    gain_here = reorder(gain.reshape(n_x * n_z, chip_rows), xz_order).reshape(-1)
    mean_square = jnp.mean(features * features, -1, keepdims=True)
    normed = (features * lax.rsqrt(mean_square + norm_eps) * gain_here).astype(bf16)
    turned_own = dot(normed, basis_own.reshape(feats, rows), 1, 0)
    turned_other = dot(normed, basis_other.reshape(feats, rows), 1, 0)
    turned = by_core(core, turned_own, turned_other, 1) * (-learn_rate)
    token_side = jnp.concatenate([normed[:, :chip_rows], turned.astype(bf16)], 1)
    token_side = jnp.stack(gather_pieces(token_side, "zl"), 0)
    token_side = jnp.stack(gather_pieces(token_side, "y"), 0)
    other_side = swap(token_side)
    token_side = jnp.stack(
        [
            jnp.where(core == 0, token_side, other_side),
            jnp.where(core == 0, other_side, token_side),
        ],
        2,
    )
    token_side = token_side.reshape(n_y * n_l * 2, block, -1)

    def slot_of(i, j):
        want_x = (at["x"] - i) % n_x
        want_z = (at["zh"] - j) % n_z
        step_y = (at["y"] - want_x) % n_y
        step_l = (at["zl"] - want_z // 2) % n_l
        return (step_y * n_l + step_l) * 2 + want_z % 2

    slots = [slot_of(i, j) for i in range(n_x) for j in range(n_z)]
    token_side = reorder(token_side, slots).reshape(n_tok, -1)

    seqs, steps = queries.shape[0], queries.shape[1]
    head_dim = k_cache.shape[-1]
    scaling = float(head_dim) ** (-0.5)
    query_rows = queries.reshape(seqs, -1, head_dim)
    k_old = k_cache[:, 0]
    v_old = v_cache[:, 0]
    score_old = (
        jnp.einsum("sqd,scd->sqc", query_rows, k_old, preferred_element_type=f32) * scaling
    )
    old_mask = (jnp.arange(k_old.shape[1], dtype=jnp.int32)[None, :] < cache_len[:, None])[
        :, None, :
    ]
    score_old = jnp.where(old_mask, score_old, -1e30)
    max_old = jnp.max(score_old, -1, keepdims=True)
    exp_old = jnp.where(old_mask, jnp.exp(score_old - max_old), 0.0)
    sum_old = jnp.sum(exp_old, -1, keepdims=True)
    out_old = jnp.einsum(
        "sqc,scd->sqd", exp_old.astype(bf16), v_old, preferred_element_type=f32
    )

    def rotate(pieces):
        own = sum(dot(basis_own[i], piece, 0, 0) for i, piece in enumerate(pieces))
        other = sum(dot(basis_other[i], piece, 0, 0) for i, piece in enumerate(pieces))
        left = by_core(core, own.astype(bf16), swap(other.astype(bf16)), 1)
        left = jnp.concatenate(gather_pieces(left, "y"), 1)
        left = jnp.concatenate(gather_pieces(left, "zl"), 1)
        return dot(left, right_in, 1, 0)

    rot_g = rotate(grad_pieces)
    rot_m = rotate(moment_pieces)
    variance_new = beta_two * variance + (1.0 - beta_two) * rot_g * rot_g
    corr_one = 1.0 - beta_one**adam_step
    corr_two = 1.0 - beta_two**adam_step
    direction = (rot_m / corr_one / (jnp.sqrt(variance_new / corr_two) + adam_eps)).astype(bf16)

    direction = jnp.stack(gather_pieces(direction, "y"), 0)
    direction = jnp.stack(gather_pieces(direction, "zl"), 0).reshape(n_l * n_y, rows, cols)
    back = lax.dot_general(
        jnp.swapaxes(direction, 0, 1).reshape(rows, -1),
        jnp.swapaxes(right_out, 0, 1).reshape(cols, -1),
        (((1,), (1,)), ((), ())),
        preferred_element_type=f32,
    ).astype(bf16)
    back_parts = back.reshape(rows, 2, half)
    back_own = pick(back_parts, core, 1)
    back_other = swap(pick(back_parts, 1 - core, 1))

    master_half = chip_halves(master.astype(bf16))
    step_side = jnp.concatenate([master_half, by_core(core, back_own, back_other, 0)], 0)
    kv = dot(token_side, step_side, 1, 0)
    kv = sum(scatter_pieces(kv.reshape(n_x, -1, half), "x"))
    kv = sum(scatter_pieces(kv.reshape(n_z, -1, half), "zh")).reshape(2, -1, half)
    key_value = by_core(core, pick(kv, core, 0), swap(pick(kv, 1 - core, 0)), 1)

    update = dot(basis_own.reshape(feats, rows), back_own, 1, 0)
    update = update + dot(basis_other.reshape(feats, rows), back_other, 1, 0)
    update = scatter_pieces(update.astype(bf16).reshape(n_x, -1, half), "x")
    update = sum(piece.astype(f32) for piece in update)
    update = scatter_pieces(update.astype(bf16).reshape(n_z, -1, half), "zh")
    update = sum(piece.astype(f32) for piece in update).reshape(2, rows, half)
    update = by_core(core, pick(update, core, 0), swap(pick(update, 1 - core, 0)), 1)

    key_value = key_value.reshape(seqs, steps, 2, head_dim)
    positions = cache_len[:, None] + jnp.arange(steps, dtype=jnp.int32)[None, :]
    k_new = rotary(key_value[:, :, 0], positions).astype(bf16)
    v_new = key_value[:, :, 1].astype(bf16)
    score_new = (
        jnp.einsum("sqd,sjd->sqj", query_rows, k_new, preferred_element_type=f32) * scaling
    )
    group = query_rows.shape[1] // steps
    query_step = jnp.arange(query_rows.shape[1], dtype=jnp.int32) // group
    new_mask = (jnp.arange(steps, dtype=jnp.int32)[None, :] <= query_step[:, None])[None]
    score_new = jnp.where(new_mask, score_new, -1e30)
    row_max = jnp.maximum(max_old, jnp.max(score_new, -1, keepdims=True))
    exp_new = jnp.where(new_mask, jnp.exp(score_new - row_max), 0.0)
    shrink = jnp.exp(max_old - row_max)
    total = sum_old * shrink + jnp.sum(exp_new, -1, keepdims=True)
    out_new = jnp.einsum(
        "sqj,sjd->sqd", exp_new.astype(bf16), v_new, preferred_element_type=f32
    )
    attended = (out_old * shrink + out_new) / total
    return (update, moment_new, variance_new, attended.reshape(seqs, steps, -1))


def solution(mesh):
    fine = Mesh(mesh.devices.reshape([SIZES[name] for name in AXES]), AXES)
    fsdp = ("x", "zh", "c")
    tp = ("zl", "y")
    in_specs = (
        P(fsdp, tp),
        P(fsdp, tp),
        P(fsdp, tp),
        P(fsdp, tp),
        P(None, fsdp),
        P(None, tp),
        P(tp, fsdp),
        P(),
        P(),
        P(fsdp, None, tp),
        P(fsdp, tp, None, None),
        P(fsdp, tp, None, None),
        P(fsdp),
    )
    out_specs = (P(fsdp, tp), P(fsdp, tp), P(fsdp, tp), P(fsdp, None, tp))
    return jax.shard_map(shards, mesh=fine, in_specs=in_specs, out_specs=out_specs, check_vma=False)
```

```python
import functools

import jax
import jax.numpy as jnp
from jax import lax
from jax.experimental import pallas as pl
from jax.experimental.pallas import tpu as pltpu
from jax.sharding import Mesh, PartitionSpec as P

beta_one = 0.9
beta_two = 0.95
adam_eps = 1e-08
learn_rate = 0.003
adam_step = 20
norm_eps = 1e-06
rope_base = 1000000.0

AXES = ("x", "zh", "c", "zl", "y")
SIZES = {"x": 4, "zh": 4, "c": 2, "zl": 2, "y": 4}
X, Z, C, L, Y = range(5)
f32 = jnp.float32
bf16 = jnp.bfloat16
VMEM_BYTES = 48 * 1024 * 1024


def call(body, outs, position, *args, far=(), scratch=()):
    vmem = pl.BlockSpec(memory_space=pltpu.VMEM)
    return pl.pallas_call(
        body,
        out_shape=[jax.ShapeDtypeStruct(shape, kind) for shape, kind in outs],
        in_specs=[pl.BlockSpec(memory_space=pltpu.SMEM)]
        + [pl.BlockSpec(memory_space=pl.ANY)] * len(far)
        + [vmem] * len(args),
        out_specs=[vmem] * len(outs),
        scratch_shapes=list(scratch),
        compiler_params=pltpu.CompilerParams(vmem_limit_bytes=VMEM_BYTES),
    )(position, *far, *args)


def shift(array, axis, by):
    size = SIZES[axis]
    return lax.ppermute(array, axis, [(i, (i + by) % size) for i in range(size)])


def swap(array):
    return shift(array, "c", 1)


def others(array, axis):
    return [shift(array, axis, k) for k in range(1, SIZES[axis])]


def scatter(arrays, axis):
    return [shift(array, axis, -k) for k, array in enumerate(arrays) if k]


def dot(left, right, left_dim=1, right_dim=0):
    return lax.dot_general(
        left, right, (((left_dim,), (right_dim,)), ((), ())), preferred_element_type=f32
    )


def by_core(core, write):
    @pl.when(core == 0)
    def _():
        write(0)

    @pl.when(core == 1)
    def _():
        write(1)


def chip_place(pos, i, j):
    return ((pos[X] + 4 - i) % 4) * 4 + (pos[Z] + 4 - j) % 4


def group_place(pos, i, j):
    return ((pos[L] + 2 - i) % 2) * 4 + (pos[Y] + 4 - j) % 4


def prepare_body(pos, grad, moment, master, moment_new, keep, send, keep_w, send_w):
    half = grad.shape[1] // 2
    new = beta_one * moment[...] + (1.0 - beta_one) * grad[...].astype(f32)
    moment_new[...] = new
    arrays = (grad[...].astype(f32), new.astype(bf16).astype(f32))

    def write(core):
        mine = slice(core * half, (core + 1) * half)
        rest = slice((1 - core) * half, (2 - core) * half)
        for i, array in enumerate(arrays):
            keep[i] = array[:, mine].T.astype(bf16)
            send[i] = array[:, rest].T.astype(bf16)
        keep_w[...] = master[:, mine].astype(bf16)
        send_w[...] = master[:, rest].astype(bf16)

    by_core(pos[C], write)


def joined(core, which, keep, recv, out):
    width = keep.shape[-1]
    out[:, core * width : (core + 1) * width] = keep[which]
    out[:, (1 - core) * width : (2 - core) * width] = recv[which]


def pack_first_body(pos, keep, recv, out):
    by_core(pos[C], lambda core: joined(core, 0, keep, recv, out))


def pack_second_body(pos, keep, recv, g0, g1, g2, g3, wide, out):
    for i, piece in enumerate((g0, g1, g2, g3)):
        wide[:, i * piece.shape[1] : (i + 1) * piece.shape[1]] = piece[...]
    by_core(pos[C], lambda core: joined(core, 1, keep, recv, out))


def pack_third_body(pos, dep, m0, m1, m2, m3, wide):
    for i, piece in enumerate((m0, m1, m2, m3)):
        wide[:, i * piece.shape[1] : (i + 1) * piece.shape[1]] = piece[...]


def basis_copies(pos, own, other, buf, sems, group):
    size = buf.shape[1] // 16
    copies = []
    for j in range(4):
        place = pl.multiple_of(chip_place(pos, group, j) * size, size)
        slot = pl.ds((group * 4 + j) * size, size)
        for k, (ref, core) in enumerate(((own, pos[C]), (other, 1 - pos[C]))):
            copies.append(
                pltpu.make_async_copy(
                    ref.at[pl.ds(place, size), :],
                    buf.at[core, slot, :],
                    sems.at[group * 4 + j, k],
                )
            )
    return copies


def left_body(pos, own, other, p0, p1, p2, p3, keep, send, buf, both, sems):
    copies = [basis_copies(pos, own, other, buf, sems, i) for i in range(4)]
    for group in copies:
        for copy in group:
            copy.start()
    deep = buf.shape[1] // 4
    total = [None, None]
    for i, piece in enumerate((p0, p1, p2, p3)):
        for copy in copies[i]:
            copy.wait()
        for core in range(2):
            part = dot(piece[...], buf[core, i * deep : (i + 1) * deep, :])
            total[core] = part if i == 0 else total[core] + part
    for core in range(2):
        both[core] = total[core].T.astype(bf16)
    keep[...] = both[pos[C]]
    send[...] = both[1 - pos[C]]


def stack_body(pos, *refs):
    out = refs[-1]
    for i, piece in enumerate(refs[:-1]):
        out[i] = piece[...]


def group_pieces(first, second):
    a0, a1, b0, b1, b2, b3 = first + second
    for i, near in enumerate((a0, a1)):
        for j in range(4):
            yield i, j, near[j], (b0, b1, b2, b3)[j][i]


def rotate_sum(pos, right, pieces):
    half = pieces[0].shape[-1]
    total = None
    for i, j, near, far in group_pieces(pieces[:2], pieces[2:]):
        place = group_place(pos, i, j) * 2
        for value, core in ((near, pos[C]), (far, 1 - pos[C])):
            rows = pl.ds(pl.multiple_of((place + core) * half, half), half)
            part = dot(value, right[rows, :])
            total = part if total is None else total + part
    return total


def variance_body(pos, right, variance, *refs):
    rot = rotate_sum(pos, right, refs[:6])
    refs[6][...] = beta_two * variance[...] + (1.0 - beta_two) * rot * rot


def direction_body(pos, right, variance_new, *refs):
    rot = rotate_sum(pos, right, refs[:6])
    corr_one = 1.0 - beta_one**adam_step
    corr_two = 1.0 - beta_two**adam_step
    value = rot / corr_one / (jnp.sqrt(variance_new[...] / corr_two) + adam_eps)
    half = value.shape[1] // 2
    refs[6][...] = value[:, :half].astype(bf16)
    refs[7][...] = value[:, half:].astype(bf16)


def back_body(pos, turned, *refs):
    keep, send = refs[6:]
    half = keep.shape[1]
    total = None
    for i, j, near, far in group_pieces(refs[:2], refs[2:6]):
        block = turned[group_place(pos, i, j)]
        part = dot(near, block[:, :half], 1, 1) + dot(far, block[:, half:], 1, 1)
        total = part if total is None else total + part
    total = total.astype(bf16)

    def write(core):
        keep[...] = total[:, core * half : (core + 1) * half]
        send[...] = total[:, (1 - core) * half : (2 - core) * half]

    by_core(pos[C], write)


def update_body(mine, pos, own, other, back_own, back_other, o0, o1, o2, o3, buf, sems):
    size = back_own.shape[0]
    core = pos[C] if mine else 1 - pos[C]
    copies = {}
    for i in (2, 1, 3, 0):
        for j in range(4):
            place = pl.multiple_of((chip_place(pos, i, j) * 2 + core) * size, size)
            for k, ref in enumerate((own, other)):
                copies[i, j, k] = pltpu.make_async_copy(
                    ref.at[pl.ds(place, size), :],
                    buf.at[k, pl.ds((i * 4 + j) * size, size), :],
                    sems.at[i * 4 + j, k],
                )
                copies[i, j, k].start()
    for i in (2, 1, 3, 0):
        out = (o0, o1, o2, o3)[i]
        for j in range(4):
            for k in range(2):
                copies[i, j, k].wait()
        rows = slice(i * 4 * size, (i + 1) * 4 * size)
        out[...] = (
            dot(buf[0, rows, :], back_own[...]) + dot(buf[1, rows, :], back_other[...])
        ).astype(bf16)


def sum_split_body(pos, *refs):
    total = sum(ref[...].astype(f32) for ref in refs[:4])
    size = total.shape[0] // 4
    for i, out in enumerate(refs[4:]):
        out[...] = total[i * size : (i + 1) * size].astype(out.dtype)


def sum_body(pos, *refs):
    refs[4][...] = sum(ref[...].astype(f32) for ref in refs[:4])


def sum_cores_body(pos, a, b, c, d, keep, send, both):
    total = sum(ref[...].astype(f32) for ref in (a, b, c, d))
    size = keep.shape[0]
    both[0] = total[:size]
    both[1] = total[size:]
    keep[...] = both[pos[C]]
    send[...] = both[1 - pos[C]]


def finish_body(pos, a, b, c, d, recv, out):
    total = sum(ref[...].astype(f32) for ref in (a, b, c, d))
    half = total.shape[1]

    def write(core):
        out[:, core * half : (core + 1) * half] = total
        out[:, (1 - core) * half : (2 - core) * half] = recv[...]

    by_core(pos[C], write)


def choose_rows_body(pos, arrived, owner, keep, send, both):
    total = None
    for i in range(8):
        part = jnp.where(owner[...] == i, arrived[i].astype(f32), 0.0)
        total = part if total is None else total + part
    size = keep.shape[0]
    both[0] = total[:size].astype(bf16)
    both[1] = total[size:].astype(bf16)
    keep[...] = both[pos[C]]
    send[...] = both[1 - pos[C]]


def join_rows_body(pos, keep, recv, out):
    width = keep.shape[1]

    def write(core):
        out[:, core * width : (core + 1) * width] = keep[...]
        out[:, (1 - core) * width : (2 - core) * width] = recv[...]

    by_core(pos[C], write)


def wide_rows_body(pos, dep, a, b, c, d, out):
    for i, piece in enumerate((a, b, c, d)):
        out[:, i * piece.shape[1] : (i + 1) * piece.shape[1]] = piece[...]


def turn_tokens_body(pos, own, other, gain, p0, p1, p2, p3, out, buf, sems):
    copies = [basis_copies(pos, own, other, buf, sems, i) for i in range(4)]
    for group in copies:
        for copy in group:
            copy.start()
    deep = p0.shape[1]
    size = deep // 4
    square = sum(
        jnp.sum(jnp.square(piece[...].astype(f32)), -1, keepdims=True)
        for piece in (p0, p1, p2, p3)
    )
    scale = lax.rsqrt(square / (deep * 4) + norm_eps)
    total = [None, None]
    for i, piece in enumerate((p0, p1, p2, p3)):
        gains = jnp.concatenate([gain[chip_place(pos, i, j)] for j in range(4)], -1)
        normed = (piece[...].astype(f32) * scale * gains).astype(bf16)
        if i == 0:
            out[:, :size] = normed[:, :size]
        for copy in copies[i]:
            copy.wait()
        for core in range(2):
            part = dot(normed, buf[core, i * deep : (i + 1) * deep, :])
            total[core] = part if i == 0 else total[core] + part
    width = size // 2
    for core in range(2):
        out[:, size + core * width : size + (core + 1) * width] = (
            total[core] * (-learn_rate)
        ).astype(bf16)


def pair_body(pos, keep, recv, out):
    out[pos[C]] = keep[...]
    out[1 - pos[C]] = recv[...]


def kv_body(pos, t0, t1, t2, t3, w_own, w_other, b_own, b_other, o0, o1, o2, o3, side, total):
    size = w_own.shape[0]

    def write(core):
        for i, (own, other) in enumerate(((w_own, w_other), (b_own, b_other))):
            side[(2 * i + core) * size : (2 * i + core + 1) * size, :] = own[...]
            side[(2 * i + 1 - core) * size : (2 * i + 2 - core) * size, :] = other[...]

    by_core(pos[C], write)
    block = t0.shape[1]
    for j, piece in enumerate((t0, t1, t2, t3)):
        value = piece[...].reshape(4 * block, 4 * size)
        part = dot(value, side[...])
        place_x = (pos[X] + 4 - (pos[Y] + 4 - j) % 4) % 4
        for i in range(2):
            for core in range(2):
                want = ((pos[L] + 2 - i) % 2) * 2 + core
                place_z = (pos[Z] + 4 - want) % 4
                first = (2 * i + core) * block
                total[place_x, place_z] = part[first : first + block]
    for i, out in enumerate((o0, o1, o2, o3)):
        for j in range(4):
            out[j * block : (j + 1) * block, :] = total[i, j].astype(bf16)


def attend_old_body(pos, dep, query, keys, values, out, row_max, row_sum):
    seqs, rows, head_dim = query.shape
    scaling = float(head_dim) ** (-0.5)
    cells = lax.broadcasted_iota(jnp.int32, (rows, keys.shape[1]), 1)
    for s in range(seqs):
        score = dot(query[s], keys[s], 1, 1) * scaling
        inside = cells < pos[len(AXES) + s]
        score = jnp.where(inside, score, -1e30)
        top = jnp.max(score, -1, keepdims=True)
        value = jnp.where(inside, jnp.exp(score - top), 0.0)
        out[s] = dot(value.astype(bf16), values[s])
        row_max[s] = jnp.broadcast_to(top, (rows, head_dim))
        row_sum[s] = jnp.broadcast_to(jnp.sum(value, -1, keepdims=True), (rows, head_dim))


def attend_new_body(
    pos, keep, recv, cosine, sine_part, query, old, row_max, row_sum, out, both, *, steps
):
    seqs, rows, head_dim = query.shape
    scaling = float(head_dim) ** (-0.5)
    both[pos[C]] = keep[...]
    both[1 - pos[C]] = recv[...]
    keys = both[0]
    half = head_dim // 2
    turned = jnp.concatenate([keys[:, half:], keys[:, :half]], 1)
    keys = (keys * cosine[...] + turned * sine_part[...]).astype(bf16)
    values = both[1].astype(bf16)
    count = keys.shape[0]
    cells = lax.broadcasted_iota(jnp.int32, (rows, count), 1)
    row_ids = lax.broadcasted_iota(jnp.int32, (rows, count), 0)
    query_step = sum((row_ids >= t * (rows // steps)).astype(jnp.int32) for t in range(1, steps))
    for s in range(seqs):
        score = dot(query[s], keys, 1, 1) * scaling
        inside = (cells >= s * steps) & (cells <= s * steps + query_step)
        score = jnp.where(inside, score, -1e30)
        top = row_max[s]
        new_top = jnp.maximum(top, jnp.max(score, -1, keepdims=True))
        shrink = jnp.exp(top - new_top)
        value = jnp.where(inside, jnp.exp(score - new_top[:, :1]), 0.0)
        total = row_sum[s] * shrink + jnp.sum(value, -1, keepdims=True)
        out[s] = (old[s] * shrink + dot(value.astype(bf16), values)) / total


def group_gather(position, first, second):
    rows, half = first.shape
    near = others(first, "y")
    far = shift(second, "zl", 1)
    (near,) = call(stack_body, [((4, rows, half), bf16)], position, first, *near)
    (far,) = call(stack_body, [((2, rows, half), bf16)], position, second, far)
    return [near, shift(near, "zl", 1), far] + others(far, "y")


def shards(
    master,
    grad,
    moment,
    variance,
    q_left,
    q_right,
    embed,
    gain,
    token_ids,
    queries,
    k_cache,
    v_cache,
    cache_len,
):
    axis_places = jnp.stack([lax.axis_index(name) for name in AXES]).astype(jnp.int32)
    position = jnp.concatenate([axis_places, cache_len])
    group_at = lax.axis_index(("zl", "y"))
    rows, cols = grad.shape
    half = cols // 2
    chip_rows = 2 * rows
    flat = (rows, half)
    turned = (half, rows)
    basis_buf = pltpu.VMEM((2, 32 * rows, rows), bf16)
    basis_sems = pltpu.SemaphoreType.DMA((16, 2))

    moment_new, keep, send, keep_w, send_w = call(
        prepare_body,
        [(grad.shape, f32), ((2,) + turned, bf16), ((2,) + turned, bf16), (flat, bf16), (flat, bf16)],
        position,
        grad,
        moment,
        master,
    )
    recv = swap(send)
    (grad_z,) = call(pack_first_body, [((half, chip_rows), bf16)], position, keep, recv)
    grad_x, moment_z = call(
        pack_second_body,
        [((half, 4 * chip_rows), bf16), ((half, chip_rows), bf16)],
        position,
        keep,
        recv,
        grad_z,
        *others(grad_z, "zh"),
    )
    grad_pieces = [grad_x] + others(grad_x, "x")
    (moment_x,) = call(
        pack_third_body,
        [((half, 4 * chip_rows), bf16)],
        position,
        moment_z,
        *others(moment_z, "zh"),
        far=(grad_pieces[1],),
    )
    moment_pieces = [moment_x] + others(moment_x, "x")

    q_left, _ = lax.optimization_barrier((q_left, recv))
    q_other = swap(q_left)
    recv_w = swap(send_w)

    flat_ids, _ = lax.optimization_barrier((token_ids.reshape(-1), recv))
    n_tok = flat_ids.shape[0]
    block = n_tok // 16
    vocab_rows = embed.shape[0]
    flat_ids = jnp.swapaxes(flat_ids.reshape(4, 2, n_tok // 8), 0, 1).reshape(-1)
    local_ids = jnp.clip(flat_ids - group_at * vocab_rows, 0, vocab_rows - 1)
    picked = jnp.take(embed, local_ids, axis=0).reshape(8, n_tok // 8, rows)
    arrived = lax.all_to_all(picked, ("zl", "y"), 0, 0, tiled=True)
    owner = (flat_ids // vocab_rows).reshape(8, n_tok // 8)
    owner = lax.dynamic_index_in_dim(owner, group_at, 0, keepdims=False).reshape(-1, 1)
    tok_keep, tok_send = call(
        choose_rows_body,
        [((block, rows), bf16)] * 2,
        position,
        arrived,
        owner,
        scratch=[pltpu.VMEM((2, block, rows), bf16)],
    )
    tok_recv = swap(tok_send)
    (tok_z,) = call(join_rows_body, [((block, chip_rows), bf16)], position, tok_keep, tok_recv)
    (tok_x,) = call(
        wide_rows_body,
        [((block, 4 * chip_rows), bf16)],
        position,
        tok_z,
        *others(tok_z, "zh"),
        far=(grad_x,),
    )
    (tok_side,) = call(
        turn_tokens_body,
        [((block, 2 * chip_rows), bf16)],
        position,
        gain.reshape(16, 1, chip_rows),
        tok_x,
        *others(tok_x, "x"),
        far=(q_left, q_other),
        scratch=[basis_buf, basis_sems],
    )
    (tok_side,) = call(
        pair_body, [((2,) + tok_side.shape, bf16)], position, tok_side, swap(tok_side)
    )
    (tok_side,) = call(
        stack_body, [((2,) + tok_side.shape, bf16)], position, tok_side, shift(tok_side, "zl", 1)
    )
    tok_sides = [tok_side] + others(tok_side, "y")

    seqs, steps = queries.shape[0], queries.shape[1]
    head_dim = k_cache.shape[-1]
    query_rows = queries.reshape(seqs, -1, head_dim)
    old_out, old_max, old_sum = call(
        attend_old_body,
        [(query_rows.shape, f32)] * 3,
        position,
        query_rows,
        k_cache.reshape(seqs, -1, head_dim),
        v_cache.reshape(seqs, -1, head_dim),
        far=(grad_x,),
    )
    token_at = (cache_len[:, None] + jnp.arange(steps, dtype=jnp.int32)[None, :]).reshape(-1, 1)
    inverse = rope_base ** (-(jnp.arange(head_dim // 2, dtype=f32) * 2.0 / head_dim))
    angles = token_at.astype(f32) * inverse
    cosine = jnp.concatenate([jnp.cos(angles)] * 2, 1)
    sine_part = jnp.concatenate([-jnp.sin(angles), jnp.sin(angles)], 1)

    def left_of(pieces):
        own, other = call(
            left_body,
            [(flat, bf16)] * 2,
            position,
            *pieces,
            far=(q_left, q_other),
            scratch=[basis_buf, pltpu.VMEM((2,) + flat, bf16), basis_sems],
        )
        return own, swap(other)

    left_g = left_of(grad_pieces)
    gathered = group_gather(position, *left_g)
    (variance_new,) = call(
        variance_body, [(grad.shape, f32)], position, q_right, variance, *gathered
    )
    right_in, _ = lax.optimization_barrier((q_right, left_g[0]))
    right_turned = lax.all_to_all(
        right_in.reshape(8, cols, cols), ("zl", "y"), 0, 0, tiled=True
    )
    gathered = group_gather(position, *left_of(moment_pieces))
    direction = call(
        direction_body, [(flat, bf16)] * 2, position, q_right, variance_new, *gathered
    )

    gathered = group_gather(position, *direction)
    back_own, back_send = call(
        back_body, [(flat, bf16)] * 2, position, right_turned, *gathered
    )
    back_other = swap(back_send)

    parts = call(
        kv_body,
        [((4 * block, half), bf16)] * 4,
        position,
        *[side.reshape(4, block, -1) for side in tok_sides],
        keep_w,
        recv_w,
        back_own,
        back_other,
        scratch=[pltpu.VMEM((4 * rows, half), bf16), pltpu.VMEM((4, 4, block, half), f32)],
    )
    parts = call(
        sum_split_body,
        [((block, half), bf16)] * 4,
        position,
        parts[0],
        *scatter(parts, "x"),
    )
    kv_keep, kv_send = call(
        sum_cores_body,
        [((block // 2, half), f32)] * 2,
        position,
        parts[0],
        *scatter(parts, "zh"),
        scratch=[pltpu.VMEM((2, block // 2, half), f32)],
    )

    def update_sums(mine):
        parts = call(
            functools.partial(update_body, mine),
            [((4 * rows, half), bf16)] * 4,
            position,
            back_own,
            back_other,
            far=(q_left, q_other),
            scratch=[pltpu.VMEM((2, 16 * rows, rows), bf16), basis_sems],
        )
        parts = call(
            sum_split_body, [(flat, bf16)] * 4, position, parts[0], *scatter(parts, "x")
        )
        return [parts[0]] + scatter(parts, "zh")

    sums_other = update_sums(False)
    sums_mine = update_sums(True)
    (update_send,) = call(sum_body, [(flat, f32)], position, *sums_other)
    (update,) = call(
        finish_body, [(grad.shape, f32)], position, *sums_mine, swap(update_send)
    )

    (attended,) = call(
        functools.partial(attend_new_body, steps=steps),
        [(query_rows.shape, f32)],
        position,
        kv_keep,
        swap(kv_send),
        cosine,
        sine_part,
        query_rows,
        old_out,
        old_max,
        old_sum,
        scratch=[pltpu.VMEM((2, block // 2, half), f32)],
    )
    return (update, moment_new, variance_new, attended.reshape(seqs, steps, -1))


def solution(mesh):
    fine = Mesh(mesh.devices.reshape([SIZES[name] for name in AXES]), AXES)
    fsdp = ("x", "zh", "c")
    tp = ("zl", "y")
    in_specs = (
        P(fsdp, tp),
        P(fsdp, tp),
        P(fsdp, tp),
        P(fsdp, tp),
        P(None, fsdp),
        P(None, tp),
        P(tp, fsdp),
        P(),
        P(),
        P(fsdp, None, tp),
        P(fsdp, tp, None, None),
        P(fsdp, tp, None, None),
        P(fsdp),
    )
    out_specs = (P(fsdp, tp), P(fsdp, tp), P(fsdp, tp), P(fsdp, None, tp))
    return jax.shard_map(shards, mesh=fine, in_specs=in_specs, out_specs=out_specs, check_vma=False)
```

```python
import functools

import jax
import jax.numpy as jnp
from jax import lax
from jax.experimental import pallas as pl
from jax.experimental.pallas import tpu as pltpu
from jax.sharding import Mesh, PartitionSpec as P

beta_one = 0.9
beta_two = 0.95
adam_eps = 1e-08
learn_rate = 0.003
adam_step = 20
norm_eps = 1e-06
rope_base = 1000000.0
token_unit = 2.0**-10

AXES = ("x", "zh", "c", "zl", "y")
SIZES = {"x": 4, "zh": 4, "c": 2, "zl": 2, "y": 4}
X, Z, C, L, Y = range(5)
f32 = jnp.float32
bf16 = jnp.bfloat16
VMEM_BYTES = 24 * 1024 * 1024


def call(body, outs, position, *args, far=(), deps=(), scratch=(), space=pltpu.VMEM):
    vmem = pl.BlockSpec(memory_space=pltpu.VMEM)
    return pl.pallas_call(
        body,
        out_shape=[jax.ShapeDtypeStruct(shape, kind) for shape, kind in outs],
        in_specs=[pl.BlockSpec(memory_space=pltpu.SMEM)]
        + [pl.BlockSpec(memory_space=pltpu.HBM)] * len(far)
        + [pl.BlockSpec(memory_space=pl.ANY)] * len(deps)
        + [vmem] * len(args),
        out_specs=[pl.BlockSpec(memory_space=space)] * len(outs),
        scratch_shapes=list(scratch),
        compiler_params=pltpu.CompilerParams(vmem_limit_bytes=VMEM_BYTES),
    )(position, *far, *deps, *args)


def shift(array, axis, by):
    size = SIZES[axis]
    return lax.ppermute(array, axis, [(i, (i + by) % size) for i in range(size)])


def swap(array):
    return shift(array, "c", 1)


def others(array, axis):
    return [shift(array, axis, k) for k in range(1, SIZES[axis])]


def scatter(arrays, axis):
    return [shift(array, axis, -k) for k, array in enumerate(arrays) if k]


def dot(left, right, left_dim=1, right_dim=0):
    return lax.dot_general(
        left, right, (((left_dim,), (right_dim,)), ((), ())), preferred_element_type=f32
    )


def chip_place(pos, i, j):
    return ((pos[X] + 4 - i) % 4) * 4 + (pos[Z] + 4 - j) % 4


def turn_body(array, out):
    out[...] = array[...].astype(f32).T.astype(bf16)


def moment_body(pos, grad, moment, master, moment_new, turned, low):
    new = beta_one * moment[...] + (1.0 - beta_one) * grad[...].astype(f32)
    moment_new[...] = new
    turned[...] = new.astype(bf16).astype(f32).T.astype(bf16)
    low[...] = master[...].astype(bf16)


def moment_tokens_body(pos, turned, arrived, owner, out):
    cols = turned.shape[0]
    out[:cols, :] = turned[...]
    total = None
    for i in range(8):
        part = jnp.where(owner[...] == i, arrived[i].astype(f32), 0.0)
        total = part if total is None else total + part
    out[cols:, :] = total.astype(bf16)


def wide_body(pos, *refs):
    out = refs[-1]
    for i, piece in enumerate(refs[-5:-1]):
        out[:, i * piece.shape[1] : (i + 1) * piece.shape[1]] = piece[...]


def basis_body(pos, own, other, out, sems):
    size = out.shape[1] // 2

    def copies(n):
        place = pl.multiple_of((chip_place(pos, n // 4, n % 4) * 2 + pos[C]) * size, size)
        slot = pl.ds(pl.multiple_of(n * size, size), size)
        return [
            pltpu.make_async_copy(
                ref.at[pl.ds(place, size), :], out.at[slot, pl.ds(k * size, size)], sems.at[n, k]
            )
            for k, ref in enumerate((own, other))
        ]

    def start(n, carry):
        for copy in copies(n):
            copy.start()
        return carry

    def wait(n, carry):
        for copy in copies(n):
            copy.wait()
        return carry

    lax.fori_loop(0, 16, start, 0)
    lax.fori_loop(0, 16, wait, 0)


def basis_parts(basis, buf, sems, order):
    deep = buf.shape[0] // 4
    copies = {}
    for i in order:
        part = pl.ds(i * deep, deep)
        copies[i] = pltpu.make_async_copy(basis.at[part, :], buf.at[part, :], sems.at[i])
        copies[i].start()

    def read(i):
        copies[i].wait()
        return buf[i * deep : (i + 1) * deep, :]

    return read


def left_body(pos, basis, dep, p0, p1, top, low, p3, keep, send, buf, sems):
    size = keep.shape[1]
    read = basis_parts(basis, buf, sems, (0, 1, 3, 2))
    total = None
    for i, piece in ((0, p0[...]), (1, p1[...]), (3, p3[...]), (2, None)):
        if piece is None:
            piece = jnp.concatenate([top[...], low[...]], 0)
        part = dot(piece, read(i))
        total = part if total is None else total + part
    keep[...] = total[:, :size]
    send[...] = total[:, size:]


def left_tokens_body(
    pos, basis, dep, gain, p0, p1, top, low, p3, keep, send, buf, sems, turned, first, square
):
    cols = size = send.shape[1]
    read = basis_parts(basis, buf, sems, (0, 1, 3, 2))
    n_tok = p0.shape[0] - cols
    squares = 0.0
    total = None
    for i, piece in ((0, p0[...]), (1, p1[...]), (3, p3[...]), (2, None)):
        if piece is None:
            piece = jnp.concatenate([top[...], low[...]], 0)
        gains = jnp.concatenate([gain[chip_place(pos, i, j) * 2 + pos[C]] for j in range(4)], -1)
        feats = piece[cols:, :].astype(f32)
        squares = squares + jnp.sum(feats * feats, -1, keepdims=True)
        feats = feats * gains * token_unit
        if i == 0:
            first[...] = feats[:, :size].reshape(first.shape)
        piece = jnp.concatenate([piece[:cols, :], feats.astype(bf16)], 0)
        part = dot(piece, read(i))
        total = part if total is None else total + part
    keep[:cols, :] = total[:cols, :size]
    send[:cols, :] = total[:cols, size:]
    for k in range(2):
        turned[k] = total[cols:, k * size : (k + 1) * size].reshape(2, n_tok // 2, size)
    square[...] = jnp.broadcast_to(squares, (n_tok, size)).reshape(square.shape)
    rows = n_tok // 2
    core = pos[C]
    for out, which, order in ((keep, core, (1, 0)), (send, 1 - core, (0, 1))):
        at = cols
        for value in (turned[order[0], which], turned[order[1], which], first[which], square[which]):
            out[at : at + rows, :] = value
            at += rows


def left_sum_body(pos, keep, recv, out):
    out[...] = (keep[...] + recv[...]).T.astype(bf16)


def pair_body(pos, here, there, out):
    out[0] = here[...]
    out[1] = there[...]


def left_tokens_sum_body(pos, keep, recv, all_out, out):
    cols = keep.shape[1]
    rows = (out.shape[0] - cols) // 4
    out[:cols, :] = (keep[:cols, :] + recv[:cols, :]).T.astype(bf16)
    parts = [slice(cols + k * rows, cols + (k + 1) * rows) for k in range(4)]
    square = keep[parts[3], :] + recv[parts[3], :]
    scale = lax.rsqrt(square / (32 * cols) + norm_eps) * (1.0 / token_unit)
    turned_other = keep[parts[0], :] + recv[parts[0], :]
    turned_own = keep[parts[1], :] + recv[parts[1], :]
    values = (
        keep[parts[2], :] * scale,
        recv[parts[2], :] * scale,
        turned_own * scale * (-learn_rate),
        turned_other * scale * (-learn_rate),
    )
    for part, value in zip(parts, values):
        out[part, :] = value.astype(bf16)
    for n in range(8):
        all_out[n] = out[...]


def variance_body(pos, right, variance, s0, s1, s2, s3, out):
    cols = right.shape[1]
    rot = None
    for j, piece in enumerate((s0, s1, s2, s3)):
        for i in range(2):
            place = ((pos[L] + 2 - i) % 2) * 4 + (pos[Y] + 4 - j) % 4
            rows = pl.ds(pl.multiple_of(place * cols, cols), cols)
            part = dot(piece[i], right[rows, :])
            rot = part if rot is None else rot + part
    out[...] = beta_two * variance[...] + (1.0 - beta_two) * rot * rot


def direction_body(pos, right, variance_new, left, out):
    cols = right.shape[1]
    rot = None
    for n in range(8):
        part = dot(left[n, :cols, :], right[n * cols : (n + 1) * cols, :])
        rot = part if rot is None else rot + part
    corr_one = 1.0 - beta_one**adam_step
    corr_two = 1.0 - beta_two**adam_step
    value = rot / corr_one / (jnp.sqrt(variance_new[...] / corr_two) + adam_eps)
    value = value.astype(bf16)
    for n in range(8):
        out[n] = dot(value, right[n * cols : (n + 1) * cols, :], 1, 1).astype(bf16)


def back_body(pos, parts, out):
    out[...] = sum(parts[n].astype(f32) for n in range(8)).astype(bf16)


def update_far_body(pos, basis, back_own, back_other, kv, top, low, buf, sems, whole):
    update_body((2,), pos, basis, back_own, back_other, kv, whole, buf, sems)
    half = top.shape[0]
    top[...] = whole[:half, :]
    low[...] = whole[half:, :]


def add_halves_body(pos, one, three, top, low, o1, o3):
    half = top.shape[0]
    o1[:half, :] = (one[:half, :].astype(f32) + top[...].astype(f32)).astype(bf16)
    o1[half:, :] = one[half:, :]
    o3[:half, :] = three[:half, :]
    o3[half:, :] = (three[half:, :].astype(f32) + low[...].astype(f32)).astype(bf16)


def update_body(steps, pos, basis, back_own, back_other, kv, *refs):
    size = back_own.shape[0]
    rows = kv.shape[2]
    back = jnp.concatenate([back_own[...], back_other[...]], 0)
    read = basis_parts(basis, refs[-2], refs[-1], steps)
    for i, out in zip(steps, refs):
        part = read(i)
        for n in range(0, 4, 2):
            rows_here = slice(n * size, (n + 2) * size)
            out[rows_here, :] = dot(part[rows_here, :], back).astype(bf16)
        for j in range(4):
            out[4 * size + j * rows : 4 * size + (j + 1) * rows, :] = kv[i, j]


def kv_body(pos, w_own, w_other, b_own, b_other, left, total):
    size = w_own.shape[0]
    many = (left.shape[1] - size) // 4
    rows = many // 2
    value = None
    for k, ref in enumerate((w_own, w_other, b_own, b_other)):
        part = slice(size + k * many, size + (k + 1) * many)
        part = dot(jnp.concatenate([left[n, part, :] for n in range(8)], 0), ref[...])
        value = part if value is None else value + part
    for n in range(8):
        step_x = (pos[X] + 4 - n % 4) % 4
        for low in range(2):
            step_z = (pos[Z] + 4 - (n // 4) * 2 - low) % 4
            first = (2 * n + low) * rows
            total[step_x, step_z] = value[first : first + rows].astype(bf16)


def sums_body(pos, a, b, c, keep, o1, o2, o3):
    rows = o1.shape[0] - o1.shape[1]
    size = o1.shape[0] - rows
    refs = (a, b, c)
    for j, out in enumerate((keep, o1, o2, o3)):
        for to, at, many in ((0, j * size, size), (size, 4 * size + j * rows, rows)):
            total = sum(ref[at : at + many, :].astype(f32) for ref in refs)
            out[to : to + many, :] = total.astype(out.dtype)


def attend_old_body(pos, dep, query, keys, values, out, row_max, row_sum):
    seqs, rows, head_dim = query.shape
    scaling = float(head_dim) ** (-0.5)
    cells = lax.broadcasted_iota(jnp.int32, (rows, keys.shape[1]), 1)
    for s in range(seqs):
        score = dot(query[s], keys[s], 1, 1) * scaling
        inside = cells < pos[len(AXES) + s]
        score = jnp.where(inside, score, -1e30)
        top = jnp.max(score, -1, keepdims=True)
        value = jnp.where(inside, jnp.exp(score - top), 0.0)
        out[s] = dot(value.astype(bf16), values[s])
        row_max[s] = jnp.broadcast_to(top, (rows, head_dim))
        row_sum[s] = jnp.broadcast_to(jnp.sum(value, -1, keepdims=True), (rows, head_dim))


def finish_body(
    pos, kept, one, two, three, cosine, sine_part, query, old, row_max, row_sum, update, out, stage
):
    size = update.shape[0]
    total = kept[...] + sum(ref[...].astype(f32) for ref in (one, two, three))
    update[...] = total[:size]
    total = total[size:]
    steps = out.shape[1]
    seqs, rows, head_dim = query.shape
    scaling = float(head_dim) ** (-0.5)
    count = total.shape[0]
    keys = total[:, :head_dim]
    values = total[:, head_dim:].astype(bf16)
    half = head_dim // 2
    turned = jnp.concatenate([keys[:, half:], keys[:, :half]], 1)
    keys = (keys * cosine[...] + turned * sine_part[...]).astype(bf16)
    cells = lax.broadcasted_iota(jnp.int32, (rows, count), 1)
    row_ids = lax.broadcasted_iota(jnp.int32, (rows, count), 0)
    query_step = sum((row_ids >= t * (rows // steps)).astype(jnp.int32) for t in range(1, steps))
    for s in range(seqs):
        score = dot(query[s], keys, 1, 1) * scaling
        inside = (cells >= s * steps) & (cells <= s * steps + query_step)
        score = jnp.where(inside, score, -1e30)
        top = row_max[s]
        new_top = jnp.maximum(top, jnp.max(score, -1, keepdims=True))
        shrink = jnp.exp(top - new_top)
        value = jnp.where(inside, jnp.exp(score - new_top[:, :1]), 0.0)
        sums = row_sum[s] * shrink + jnp.sum(value, -1, keepdims=True)
        stage[...] = (old[s] * shrink + dot(value.astype(bf16), values)) / sums
        group = rows // steps
        for g in range(group):
            out[s, :, g * head_dim : (g + 1) * head_dim] = stage[g::group, :]


def exchange(array):
    return lax.all_to_all(array, ("zl", "y"), 0, 0, tiled=True)


def ring_first(array):
    half = array.shape[0] // 2
    one, three = shift(array, "x", 1), shift(array, "x", -1)
    return one, three, one[:half], three[half:]


def ring_gather(array, first):
    one, three, top, low = first
    return [array, one, shift(top, "x", 1), shift(low, "x", -1), three]


def after(array, *deps):
    return lax.optimization_barrier((array,) + deps)[0]


def shards(
    master,
    grad,
    moment,
    variance,
    q_left,
    q_right,
    embed,
    gain,
    token_ids,
    queries,
    k_cache,
    v_cache,
    cache_len,
):
    axis_places = jnp.stack([lax.axis_index(name) for name in AXES]).astype(jnp.int32)
    position = jnp.concatenate([axis_places, cache_len])
    group_at = lax.axis_index(("zl", "y"))
    rows, cols = grad.shape
    square = (rows, cols)

    grad_t = pl.pallas_call(
        turn_body,
        out_shape=jax.ShapeDtypeStruct((cols, rows), bf16),
        compiler_params=pltpu.CompilerParams(vmem_limit_bytes=VMEM_BYTES),
    )(grad)
    grad_z = others(grad_t, "zh")

    flat_ids = token_ids.reshape(4, 2, 2, 2, -1)
    tok_rows = flat_ids.shape[-1]
    flat_ids = after(jnp.transpose(flat_ids, (1, 0, 3, 2, 4)).reshape(-1), grad_z[0])
    n_tok = flat_ids.shape[0]
    vocab_rows = embed.shape[0]
    local_ids = jnp.clip(flat_ids - group_at * vocab_rows, 0, vocab_rows - 1)
    picked = embed.at[local_ids].get(mode="promise_in_bounds").reshape(8, n_tok // 8, rows)
    arrived = exchange(picked)
    owner = (flat_ids // vocab_rows).reshape(8, n_tok // 8)
    owner = lax.dynamic_index_in_dim(owner, group_at, 0, keepdims=False).reshape(-1, 1)

    q_other = swap(after(q_left, grad_t))
    (basis,) = call(
        basis_body,
        [((16 * rows, 2 * rows), bf16)],
        position,
        far=(q_left, q_other),
        scratch=[pltpu.SemaphoreType.DMA((16, 2))],
        space=pltpu.HBM,
    )
    basis_scratch = [pltpu.VMEM(basis.shape, bf16), pltpu.SemaphoreType.DMA((4,))]
    moment_new, moment_t, master_low = call(
        moment_body,
        [(square, f32), ((cols, rows), bf16), (square, bf16)],
        position,
        after(grad, grad_t),
        moment,
        master,
    )
    deep = cols + n_tok // 8
    (grad_x,) = call(wide_body, [((cols, 4 * rows), bf16)], position, grad_t, *grad_z, deps=(picked, q_other))
    grad_first = ring_first(grad_x)
    grad_pieces = ring_gather(grad_x, grad_first)
    (moment_z,) = call(
        moment_tokens_body,
        [((deep, rows), bf16)],
        position,
        moment_t,
        arrived,
        owner,
    )
    moment_z = after(moment_z, grad_x)
    moment_others = others(moment_z, "zh")
    (moment_x,) = call(
        wide_body, [((deep, 4 * rows), bf16)], position, moment_z, *moment_others, deps=(*grad_pieces[2:4], basis)
    )
    moment_first = ring_first(moment_x)
    moment_pieces = ring_gather(moment_x, moment_first)

    master_other = swap(master_low)

    seqs, steps = queries.shape[0], queries.shape[1]
    head_dim = k_cache.shape[-1]
    query_rows = queries.reshape(seqs, -1, head_dim)
    old_out, old_max, old_sum = call(
        attend_old_body,
        [(query_rows.shape, f32)] * 3,
        position,
        query_rows,
        k_cache.reshape(seqs, -1, head_dim),
        v_cache.reshape(seqs, -1, head_dim),
        deps=(moment_others[0],),
    )
    token_at = (cache_len[:, None] + jnp.arange(steps, dtype=jnp.int32)[None, :]).reshape(-1, 1)
    inverse = rope_base ** (-(jnp.arange(head_dim // 2, dtype=f32) * 2.0 / head_dim))
    angles = after(token_at, moment_others[0]).astype(f32) * inverse
    cosine = jnp.concatenate([jnp.cos(angles)] * 2, 1)
    sine_part = jnp.concatenate([-jnp.sin(angles), jnp.sin(angles)], 1)

    keep, send = call(
        left_body,
        [((cols, rows), f32)] * 2,
        position,
        *grad_pieces,
        far=(basis,),
        deps=(moment_x,),
        scratch=basis_scratch,
    )
    (left_g,) = call(left_sum_body, [(square, bf16)], position, keep, swap(send))
    (left_g,) = call(
        pair_body, [((2,) + square, bf16)], position, left_g, shift(left_g, "zl", 1)
    )
    (variance_new,) = call(
        variance_body, [(square, f32)], position, q_right, variance, left_g, *others(left_g, "y")
    )

    keep, send = call(
        left_tokens_body,
        [((cols + n_tok // 4, rows), f32)] * 2,
        position,
        gain.reshape(32, 1, rows),
        *moment_pieces,
        far=(basis,),
        deps=(variance_new,),
        scratch=basis_scratch
        + [
            pltpu.VMEM((2, 2, n_tok // 16, rows), f32),
            pltpu.VMEM((2, n_tok // 16, rows), f32),
            pltpu.VMEM((2, n_tok // 16, rows), f32),
        ],
    )
    (left_m,) = call(
        left_tokens_sum_body,
        [((8, cols + n_tok // 4, rows), bf16)],
        position,
        keep,
        swap(send),
        scratch=[pltpu.VMEM((cols + n_tok // 4, rows), bf16)],
    )
    left_m = exchange(left_m)

    (parts,) = call(
        direction_body, [((8,) + square, bf16)], position, q_right, variance_new, left_m
    )
    (back_own,) = call(back_body, [(square, bf16)], position, exchange(parts))
    back_other = swap(back_own)

    (kv,) = call(
        kv_body,
        [((4, 4, tok_rows, cols), bf16)],
        position,
        master_low,
        master_other,
        back_own,
        back_other,
        left_m,
    )

    many = 4 * (rows + tok_rows)
    top, low = call(
        update_far_body,
        [((many // 2, cols), bf16)] * 2,
        position,
        back_own,
        back_other,
        kv,
        far=(basis,),
        scratch=basis_scratch + [pltpu.VMEM((many, cols), bf16)],
    )
    top, low = shift(top, "x", -1), shift(low, "x", 1)
    one, three, zero = call(
        functools.partial(update_body, (1, 3, 0)),
        [((many, cols), bf16)] * 3,
        position,
        back_own,
        back_other,
        kv,
        far=(basis,),
        scratch=basis_scratch,
    )
    one, three = call(
        add_halves_body, [((many, cols), bf16)] * 2, position, one, three, top, low
    )
    parts = call(
        sums_body,
        [((rows + tok_rows, cols), f32)] + [((rows + tok_rows, cols), bf16)] * 3,
        position,
        zero,
        shift(one, "x", -1),
        shift(three, "x", 1),
    )
    update, attended = call(
        finish_body,
        [(square, f32), (queries.shape, f32)],
        position,
        parts[0],
        *scatter(parts, "zh"),
        cosine,
        sine_part,
        query_rows,
        old_out,
        old_max,
        old_sum,
        scratch=[pltpu.VMEM(query_rows.shape[1:], f32)],
    )
    return (update, moment_new, variance_new, attended)


def solution(mesh):
    fine = Mesh(mesh.devices.reshape([SIZES[name] for name in AXES]), AXES)
    fsdp = ("x", "zh", "c")
    tp = ("zl", "y")
    in_specs = (
        P(fsdp, tp),
        P(fsdp, tp),
        P(fsdp, tp),
        P(fsdp, tp),
        P(None, fsdp),
        P(None, tp),
        P(tp, fsdp),
        P(),
        P(),
        P(fsdp, None, tp),
        P(fsdp, tp, None, None),
        P(fsdp, tp, None, None),
        P(fsdp),
    )
    out_specs = (P(fsdp, tp), P(fsdp, tp), P(fsdp, tp), P(fsdp, None, tp))
    return jax.shard_map(shards, mesh=fine, in_specs=in_specs, out_specs=out_specs, check_vma=False)
```

```python
import functools

import jax
import jax.numpy as jnp
from jax import lax
from jax.experimental import pallas as pl
from jax.experimental.pallas import tpu as pltpu
from jax.sharding import Mesh, PartitionSpec as P

beta_one = 0.9
beta_two = 0.95
adam_eps = 1e-08
learn_rate = 0.003
adam_step = 20
norm_eps = 1e-06
rope_base = 1000000.0
token_unit = 2.0**-10

AXES = ("x", "zh", "c", "zl", "y")
SIZES = {"x": 4, "zh": 4, "c": 2, "zl": 2, "y": 4}
X, Z, C, L, Y = range(5)
f32 = jnp.float32
bf16 = jnp.bfloat16
VMEM_BYTES = 20 * 1024 * 1024


def call(body, outs, position, *args, far=(), deps=(), scratch=(), space=pltpu.VMEM):
    vmem = pl.BlockSpec(memory_space=pltpu.VMEM)
    return pl.pallas_call(
        body,
        out_shape=[jax.ShapeDtypeStruct(shape, kind) for shape, kind in outs],
        in_specs=[pl.BlockSpec(memory_space=pltpu.SMEM)]
        + [pl.BlockSpec(memory_space=pltpu.HBM)] * len(far)
        + [pl.BlockSpec(memory_space=pl.ANY)] * len(deps)
        + [vmem] * len(args),
        out_specs=[pl.BlockSpec(memory_space=space)] * len(outs),
        scratch_shapes=list(scratch),
        compiler_params=pltpu.CompilerParams(vmem_limit_bytes=VMEM_BYTES),
    )(position, *far, *deps, *args)


def shift(array, axis, by):
    size = SIZES[axis]
    return lax.ppermute(array, axis, [(i, (i + by) % size) for i in range(size)])


def swap(array):
    return shift(array, "c", 1)


def others(array, axis):
    return [shift(array, axis, k) for k in range(1, SIZES[axis])]


def scatter(arrays, axis):
    return [shift(array, axis, -k) for k, array in enumerate(arrays) if k]


def dot(left, right, left_dim=1, right_dim=0):
    return lax.dot_general(
        left, right, (((left_dim,), (right_dim,)), ((), ())), preferred_element_type=f32
    )


def chip_place(pos, i, j):
    return ((pos[X] + 4 - i) % 4) * 4 + (pos[Z] + 4 - j) % 4


def turn_body(array, out):
    out[...] = array[...].astype(f32).T.astype(bf16)


def moment_body(pos, grad, moment, master, moment_new, turned, low):
    new = beta_one * moment[...] + (1.0 - beta_one) * grad[...].astype(f32)
    moment_new[...] = new
    turned[...] = new.astype(bf16).astype(f32).T.astype(bf16)
    low[...] = master[...].astype(bf16)


def moment_tokens_body(pos, turned, arrived, owner, out):
    cols = turned.shape[0]
    out[:cols, :] = turned[...]
    total = None
    for i in range(8):
        part = jnp.where(owner[...] == i, arrived[i].astype(f32), 0.0)
        total = part if total is None else total + part
    out[cols:, :] = total.astype(bf16)


def wide_body(pos, *refs):
    out = refs[-1]
    for i, piece in enumerate(refs[-5:-1]):
        out[:, i * piece.shape[1] : (i + 1) * piece.shape[1]] = piece[...]


def basis_body(pos, own, other, b0, b1, b2, b3, sems):
    size = b0.shape[1] // 2

    def copies(out, i, j):
        place = pl.multiple_of((chip_place(pos, i, j) * 2 + pos[C]) * size, size)
        slot = pl.ds(pl.multiple_of(j * size, size), size)
        return [
            pltpu.make_async_copy(
                ref.at[pl.ds(place, size), :], out.at[slot, pl.ds(k * size, size)], sems.at[i, j, k]
            )
            for k, ref in enumerate((own, other))
        ]

    outs = tuple(enumerate((b0, b1, b2, b3)))
    for i, out in outs:

        def start(j, carry, i=i, out=out):
            for copy in copies(out, i, j):
                copy.start()
            return carry

        lax.fori_loop(0, 4, start, 0)
    for i, out in outs:

        def wait(j, carry, i=i, out=out):
            for copy in copies(out, i, j):
                copy.wait()
            return carry

        lax.fori_loop(0, 4, wait, 0)


def left_body(pos, dep, b0, b1, b2, b3, p0, p1, top, low, p3, keep, send):
    size = keep.shape[1]
    total = None
    for basis, piece in ((b0, p0[...]), (b1, p1[...]), (b3, p3[...]), (b2, None)):
        if piece is None:
            piece = jnp.concatenate([top[...], low[...]], 0)
        part = dot(piece, basis[...])
        total = part if total is None else total + part
    keep[...] = total[:, :size].astype(bf16)
    send[...] = total[:, size:].astype(bf16)


def left_tokens_body(
    pos, dep_a, dep_b, b0, b1, b2, b3, gain, p0, p1, top, low, p3, keep, send, turned, first, square
):
    cols = size = send.shape[1]
    parts = (b0, b1, b2, b3)
    n_tok = p0.shape[0] - cols
    squares = 0.0
    total = None
    for i, piece in ((0, p0[...]), (1, p1[...]), (3, p3[...]), (2, None)):
        if piece is None:
            piece = jnp.concatenate([top[...], low[...]], 0)
        gains = jnp.concatenate([gain[chip_place(pos, i, j) * 2 + pos[C]] for j in range(4)], -1)
        feats = piece[cols:, :].astype(f32)
        squares = squares + jnp.sum(feats * feats, -1, keepdims=True)
        feats = feats * gains * token_unit
        if i == 0:
            first[...] = feats[:, :size].reshape(first.shape)
        piece = jnp.concatenate([piece[:cols, :], feats.astype(bf16)], 0)
        part = dot(piece, parts[i][...])
        total = part if total is None else total + part
    keep[:cols, :] = total[:cols, :size]
    send[:cols, :] = total[:cols, size:]
    for k in range(2):
        turned[k] = total[cols:, k * size : (k + 1) * size].reshape(2, n_tok // 2, size)
    square[...] = jnp.broadcast_to(squares, (n_tok, size)).reshape(square.shape)
    rows = n_tok // 2
    core = pos[C]
    for out, which, order in ((keep, core, (1, 0)), (send, 1 - core, (0, 1))):
        at = cols
        for value in (turned[order[0], which], turned[order[1], which], first[which], square[which]):
            out[at : at + rows, :] = value
            at += rows


def pair_body(pos, keep, core, low, both, out):
    out[0] = (keep[...].astype(f32) + core[...].astype(f32)).T.astype(bf16)
    out[1] = (low[...].astype(f32) + both[...].astype(f32)).T.astype(bf16)


def left_tokens_sum_body(pos, keep, recv, all_out, out):
    cols = keep.shape[1]
    rows = (out.shape[0] - cols) // 4
    out[:cols, :] = (keep[:cols, :] + recv[:cols, :]).T.astype(bf16)
    parts = [slice(cols + k * rows, cols + (k + 1) * rows) for k in range(4)]
    square = keep[parts[3], :] + recv[parts[3], :]
    scale = lax.rsqrt(square / (32 * cols) + norm_eps) * (1.0 / token_unit)
    turned_other = keep[parts[0], :] + recv[parts[0], :]
    turned_own = keep[parts[1], :] + recv[parts[1], :]
    values = (
        keep[parts[2], :] * scale,
        recv[parts[2], :] * scale,
        turned_own * scale * (-learn_rate),
        turned_other * scale * (-learn_rate),
    )
    for part, value in zip(parts, values):
        out[part, :] = value.astype(bf16)
    for n in range(8):
        all_out[n] = out[...]


def variance_body(pos, right, variance, s0, s1, s2, s3, out):
    cols = right.shape[1]
    rot = None
    for j, piece in enumerate((s0, s1, s2, s3)):
        for i in range(2):
            place = ((pos[L] + 2 - i) % 2) * 4 + (pos[Y] + 4 - j) % 4
            rows = pl.ds(pl.multiple_of(place * cols, cols), cols)
            part = dot(piece[i], right[rows, :])
            rot = part if rot is None else rot + part
    out[...] = beta_two * variance[...] + (1.0 - beta_two) * rot * rot


def direction_body(pos, right, variance_new, left, out):
    cols = right.shape[1]
    rot = None
    for n in range(8):
        part = dot(left[n, :cols, :], right[n * cols : (n + 1) * cols, :])
        rot = part if rot is None else rot + part
    corr_one = 1.0 - beta_one**adam_step
    corr_two = 1.0 - beta_two**adam_step
    value = rot / corr_one / (jnp.sqrt(variance_new[...] / corr_two) + adam_eps)
    value = value.astype(bf16)
    for n in range(8):
        out[n] = dot(value, right[n * cols : (n + 1) * cols, :], 1, 1).astype(bf16)


def back_body(pos, parts, out):
    out[...] = sum(parts[n].astype(f32) for n in range(8)).astype(bf16)


def update_far_body(pos, back_own, back_other, kv, basis, top, low, whole):
    update_body((2,), pos, back_own, back_other, kv, basis, whole)
    half = top.shape[0]
    top[...] = whole[:half, :]
    low[...] = whole[half:, :]


def add_halves_body(pos, one, three, top, low, o1, o3):
    half = top.shape[0]
    o1[:half, :] = (one[:half, :].astype(f32) + top[...].astype(f32)).astype(bf16)
    o1[half:, :] = one[half:, :]
    o3[:half, :] = three[:half, :]
    o3[half:, :] = (three[half:, :].astype(f32) + low[...].astype(f32)).astype(bf16)


def update_body(steps, pos, back_own, back_other, kv, *refs):
    size = back_own.shape[0]
    rows = kv.shape[2]
    back = jnp.concatenate([back_own[...], back_other[...]], 0)
    many = len(steps)
    for i, basis, out in zip(steps, refs[:many], refs[many:]):
        for n in range(0, 4, 2):
            part = slice(n * size, (n + 2) * size)
            out[part, :] = dot(basis[part, :], back).astype(bf16)
        for j in range(4):
            out[4 * size + j * rows : 4 * size + (j + 1) * rows, :] = kv[i, j]


def kv_body(pos, w_own, w_other, b_own, b_other, left, total):
    size = w_own.shape[0]
    many = (left.shape[1] - size) // 4
    rows = many // 2
    value = None
    for k, ref in enumerate((w_own, w_other, b_own, b_other)):
        part = slice(size + k * many, size + (k + 1) * many)
        part = dot(jnp.concatenate([left[n, part, :] for n in range(8)], 0), ref[...])
        value = part if value is None else value + part
    for n in range(8):
        step_x = (pos[X] + 4 - n % 4) % 4
        for low in range(2):
            step_z = (pos[Z] + 4 - (n // 4) * 2 - low) % 4
            first = (2 * n + low) * rows
            total[step_x, step_z] = value[first : first + rows].astype(bf16)


def sums_body(pos, a, b, c, keep, o1, o2, o3):
    rows = o1.shape[0] - o1.shape[1]
    size = o1.shape[0] - rows
    refs = (a, b, c)
    for j, out in enumerate((keep, o1, o2, o3)):
        for to, at, many in ((0, j * size, size), (size, 4 * size + j * rows, rows)):
            total = sum(ref[at : at + many, :].astype(f32) for ref in refs)
            out[to : to + many, :] = total.astype(out.dtype)


def attend_old_body(pos, dep, query, keys, values, out, row_max, row_sum):
    seqs, rows, head_dim = query.shape
    scaling = float(head_dim) ** (-0.5)
    cells = lax.broadcasted_iota(jnp.int32, (rows, keys.shape[1]), 1)
    for s in range(seqs):
        score = dot(query[s], keys[s], 1, 1) * scaling
        inside = cells < pos[len(AXES) + s]
        score = jnp.where(inside, score, -1e30)
        top = jnp.max(score, -1, keepdims=True)
        value = jnp.where(inside, jnp.exp(score - top), 0.0)
        out[s] = dot(value.astype(bf16), values[s])
        row_max[s] = jnp.broadcast_to(top, (rows, head_dim))
        row_sum[s] = jnp.broadcast_to(jnp.sum(value, -1, keepdims=True), (rows, head_dim))


def finish_body(
    pos, kept, one, two, three, cosine, sine_part, query, old, row_max, row_sum, update, out, stage
):
    size = update.shape[0]
    total = kept[...] + sum(ref[...].astype(f32) for ref in (one, two, three))
    update[...] = total[:size]
    total = total[size:]
    steps = out.shape[1]
    seqs, rows, head_dim = query.shape
    scaling = float(head_dim) ** (-0.5)
    count = total.shape[0]
    keys = total[:, :head_dim]
    values = total[:, head_dim:].astype(bf16)
    half = head_dim // 2
    turned = jnp.concatenate([keys[:, half:], keys[:, :half]], 1)
    keys = (keys * cosine[...] + turned * sine_part[...]).astype(bf16)
    cells = lax.broadcasted_iota(jnp.int32, (rows, count), 1)
    row_ids = lax.broadcasted_iota(jnp.int32, (rows, count), 0)
    query_step = sum((row_ids >= t * (rows // steps)).astype(jnp.int32) for t in range(1, steps))
    for s in range(seqs):
        score = dot(query[s], keys, 1, 1) * scaling
        inside = (cells >= s * steps) & (cells <= s * steps + query_step)
        score = jnp.where(inside, score, -1e30)
        top = row_max[s]
        new_top = jnp.maximum(top, jnp.max(score, -1, keepdims=True))
        shrink = jnp.exp(top - new_top)
        value = jnp.where(inside, jnp.exp(score - new_top[:, :1]), 0.0)
        sums = row_sum[s] * shrink + jnp.sum(value, -1, keepdims=True)
        stage[...] = (old[s] * shrink + dot(value.astype(bf16), values)) / sums
        group = rows // steps
        for g in range(group):
            out[s, :, g * head_dim : (g + 1) * head_dim] = stage[g::group, :]


def exchange(array):
    return lax.all_to_all(array, ("zl", "y"), 0, 0, tiled=True)


def ring_first(array):
    return shift(array, "x", 1), shift(array, "x", -1)


def ring_gather(array, first, dep):
    one, three = first
    half = array.shape[0] // 2
    top, low = after(one, dep[0])[:half], after(three, dep[-1])[half:]
    return [array, one, shift(top, "x", 1), shift(low, "x", -1), three]


def after(array, *deps):
    return lax.optimization_barrier((array,) + deps)[0]


def shards(
    master,
    grad,
    moment,
    variance,
    q_left,
    q_right,
    embed,
    gain,
    token_ids,
    queries,
    k_cache,
    v_cache,
    cache_len,
):
    axis_places = jnp.stack([lax.axis_index(name) for name in AXES]).astype(jnp.int32)
    position = jnp.concatenate([axis_places, cache_len])
    group_at = lax.axis_index(("zl", "y"))
    rows, cols = grad.shape
    square = (rows, cols)

    grad_t = pl.pallas_call(
        turn_body,
        out_shape=jax.ShapeDtypeStruct((cols, rows), bf16),
        compiler_params=pltpu.CompilerParams(vmem_limit_bytes=VMEM_BYTES),
    )(grad)
    grad_z = others(grad_t, "zh")

    flat_ids = token_ids.reshape(4, 2, 2, 2, -1)
    tok_rows = flat_ids.shape[-1]
    flat_ids = after(jnp.transpose(flat_ids, (1, 0, 3, 2, 4)).reshape(-1), grad_z[0])
    n_tok = flat_ids.shape[0]
    vocab_rows = embed.shape[0]
    local_ids = jnp.clip(flat_ids - group_at * vocab_rows, 0, vocab_rows - 1)
    picked = embed.at[local_ids].get(mode="promise_in_bounds").reshape(8, n_tok // 8, rows)
    arrived = exchange(picked)
    owner = (flat_ids // vocab_rows).reshape(8, n_tok // 8)
    owner = lax.dynamic_index_in_dim(owner, group_at, 0, keepdims=False).reshape(-1, 1)

    q_other = swap(after(q_left, grad_t))
    basis = call(
        basis_body,
        [((4 * rows, 2 * rows), bf16)] * 4,
        position,
        far=(q_left, q_other),
        scratch=[pltpu.SemaphoreType.DMA((4, 4, 2))],
    )
    moment_new, moment_t, master_low = call(
        moment_body,
        [(square, f32), ((cols, rows), bf16), (square, bf16)],
        position,
        after(grad, grad_t),
        moment,
        master,
    )
    deep = cols + n_tok // 8
    (grad_x,) = call(wide_body, [((cols, 4 * rows), bf16)], position, grad_t, *grad_z, deps=(picked, q_other))
    grad_first = ring_first(grad_x)
    (moment_z,) = call(
        moment_tokens_body,
        [((deep, rows), bf16)],
        position,
        moment_t,
        arrived,
        owner,
    )
    moment_z = after(moment_z, grad_x)
    grad_pieces = ring_gather(grad_x, grad_first, [moment_z])
    moment_others = others(moment_z, "zh")
    (moment_x,) = call(
        wide_body, [((deep, 4 * rows), bf16)], position, moment_z, *moment_others, deps=(*grad_pieces[2:4], basis[0])
    )
    moment_first = ring_first(moment_x)

    master_other = swap(master_low)

    seqs, steps = queries.shape[0], queries.shape[1]
    head_dim = k_cache.shape[-1]
    query_rows = queries.reshape(seqs, -1, head_dim)
    old_out, old_max, old_sum = call(
        attend_old_body,
        [(query_rows.shape, f32)] * 3,
        position,
        query_rows,
        k_cache.reshape(seqs, -1, head_dim),
        v_cache.reshape(seqs, -1, head_dim),
        deps=(moment_others[0],),
    )
    token_at = (cache_len[:, None] + jnp.arange(steps, dtype=jnp.int32)[None, :]).reshape(-1, 1)
    inverse = rope_base ** (-(jnp.arange(head_dim // 2, dtype=f32) * 2.0 / head_dim))
    angles = after(token_at, moment_others[0]).astype(f32) * inverse
    cosine = jnp.concatenate([jnp.cos(angles)] * 2, 1)
    sine_part = jnp.concatenate([-jnp.sin(angles), jnp.sin(angles)], 1)

    keep, send = call(
        left_body,
        [((cols, rows), bf16)] * 2,
        position,
        *basis,
        *grad_pieces,
        deps=(moment_x,),
    )
    (left_g,) = call(
        pair_body,
        [((2,) + square, bf16)],
        position,
        keep,
        swap(send),
        shift(keep, "zl", 1),
        lax.ppermute(send, ("c", "zl"), [(i, 3 - i) for i in range(4)]),
    )
    left_others = others(left_g, "y")
    (variance_new,) = call(
        variance_body, [(square, f32)], position, q_right, variance, left_g, *left_others
    )

    moment_pieces = ring_gather(moment_x, moment_first, left_others[::2])
    keep, send = call(
        left_tokens_body,
        [((cols + n_tok // 4, rows), f32)] * 2,
        position,
        *basis,
        gain.reshape(32, 1, rows),
        *moment_pieces,
        deps=(variance_new, master_other),
        scratch=[
            pltpu.VMEM((2, 2, n_tok // 16, rows), f32),
            pltpu.VMEM((2, n_tok // 16, rows), f32),
            pltpu.VMEM((2, n_tok // 16, rows), f32),
        ],
    )
    (left_m,) = call(
        left_tokens_sum_body,
        [((8, cols + n_tok // 4, rows), bf16)],
        position,
        keep,
        swap(send),
        scratch=[pltpu.VMEM((cols + n_tok // 4, rows), bf16)],
    )
    left_m = exchange(left_m)

    (parts,) = call(
        direction_body, [((8,) + square, bf16)], position, q_right, variance_new, left_m
    )
    (back_own,) = call(back_body, [(square, bf16)], position, exchange(parts))
    back_other = swap(back_own)

    (kv,) = call(
        kv_body,
        [((4, 4, tok_rows, cols), bf16)],
        position,
        master_low,
        master_other,
        back_own,
        back_other,
        left_m,
    )

    many = 4 * (rows + tok_rows)
    top, low = call(
        update_far_body,
        [((many // 2, cols), bf16)] * 2,
        position,
        back_own,
        back_other,
        kv,
        basis[2],
        scratch=[pltpu.VMEM((many, cols), bf16)],
    )
    top, low = shift(top, "x", -1), shift(low, "x", 1)
    one, three, zero = call(
        functools.partial(update_body, (1, 3, 0)),
        [((many, cols), bf16)] * 3,
        position,
        back_own,
        back_other,
        kv,
        basis[1],
        basis[3],
        basis[0],
    )
    one, three = call(
        add_halves_body, [((many, cols), bf16)] * 2, position, one, three, top, low
    )
    parts = call(
        sums_body,
        [((rows + tok_rows, cols), f32)] + [((rows + tok_rows, cols), bf16)] * 3,
        position,
        zero,
        shift(one, "x", -1),
        shift(three, "x", 1),
    )
    update, attended = call(
        finish_body,
        [(square, f32), (queries.shape, f32)],
        position,
        parts[0],
        *scatter(parts, "zh"),
        cosine,
        sine_part,
        query_rows,
        old_out,
        old_max,
        old_sum,
        scratch=[pltpu.VMEM(query_rows.shape[1:], f32)],
    )
    return (update, moment_new, variance_new, attended)


def solution(mesh):
    fine = Mesh(mesh.devices.reshape([SIZES[name] for name in AXES]), AXES)
    fsdp = ("x", "zh", "c")
    tp = ("zl", "y")
    in_specs = (
        P(fsdp, tp),
        P(fsdp, tp),
        P(fsdp, tp),
        P(fsdp, tp),
        P(None, fsdp),
        P(None, tp),
        P(tp, fsdp),
        P(),
        P(),
        P(fsdp, None, tp),
        P(fsdp, tp, None, None),
        P(fsdp, tp, None, None),
        P(fsdp),
    )
    out_specs = (P(fsdp, tp), P(fsdp, tp), P(fsdp, tp), P(fsdp, None, tp))
    return jax.shard_map(shards, mesh=fine, in_specs=in_specs, out_specs=out_specs, check_vma=False)
```

```python
import functools

import jax
import jax.numpy as jnp
from jax import lax
from jax.experimental import pallas as pl
from jax.experimental.pallas import tpu as pltpu
from jax.sharding import Mesh, PartitionSpec as P

beta_one = 0.9
beta_two = 0.95
adam_eps = 1e-08
learn_rate = 0.003
adam_step = 20
norm_eps = 1e-06
rope_base = 1000000.0
token_unit = 2.0**-10

AXES = ("x", "zh", "c", "zl", "y")
SIZES = {"x": 4, "zh": 4, "c": 2, "zl": 2, "y": 4}
X, Z, C, L, Y = range(5)
f32 = jnp.float32
bf16 = jnp.bfloat16
VMEM_BYTES = 20 * 1024 * 1024


def call(body, outs, position, *args, far=(), deps=(), scratch=(), space=pltpu.VMEM):
    vmem = pl.BlockSpec(memory_space=pltpu.VMEM)
    return pl.pallas_call(
        body,
        out_shape=[jax.ShapeDtypeStruct(shape, kind) for shape, kind in outs],
        in_specs=[pl.BlockSpec(memory_space=pltpu.SMEM)]
        + [pl.BlockSpec(memory_space=pltpu.HBM)] * len(far)
        + [pl.BlockSpec(memory_space=pl.ANY)] * len(deps)
        + [vmem] * len(args),
        out_specs=[pl.BlockSpec(memory_space=space)] * len(outs),
        scratch_shapes=list(scratch),
        compiler_params=pltpu.CompilerParams(vmem_limit_bytes=VMEM_BYTES),
    )(position, *far, *deps, *args)


def shift(array, axis, by):
    size = SIZES[axis]
    return lax.ppermute(array, axis, [(i, (i + by) % size) for i in range(size)])


def swap(array):
    return shift(array, "c", 1)


def others(array, axis):
    return [shift(array, axis, k) for k in range(1, SIZES[axis])]


def scatter(arrays, axis):
    return [shift(array, axis, -k) for k, array in enumerate(arrays) if k]


def dot(left, right, left_dim=1, right_dim=0):
    return lax.dot_general(
        left, right, (((left_dim,), (right_dim,)), ((), ())), preferred_element_type=f32
    )


def chip_place(pos, i, j):
    return ((pos[X] + 4 - i) % 4) * 4 + (pos[Z] + 4 - j) % 4


def turn_body(array, out):
    out[...] = array[...].astype(f32).T.astype(bf16)


def moment_body(pos, grad, moment, master, moment_new, turned, low):
    new = beta_one * moment[...] + (1.0 - beta_one) * grad[...].astype(f32)
    moment_new[...] = new
    turned[...] = new.astype(bf16).astype(f32).T.astype(bf16)
    low[...] = master[...].astype(bf16)


def moment_tokens_body(pos, turned, arrived, owner, out):
    cols = turned.shape[0]
    out[:cols, :] = turned[...]
    total = None
    for i in range(8):
        part = jnp.where(owner[...] == i, arrived[i].astype(f32), 0.0)
        total = part if total is None else total + part
    out[cols:, :] = total.astype(bf16)


def wide_body(pos, *refs):
    out = refs[-1]
    for i, piece in enumerate(refs[-5:-1]):
        out[:, i * piece.shape[1] : (i + 1) * piece.shape[1]] = piece[...]


def basis_body(pos, own, other, b0, b1, b2, b3, sems):
    size = b0.shape[1] // 2

    def copies(out, i, j):
        place = pl.multiple_of((chip_place(pos, i, j) * 2 + pos[C]) * size, size)
        slot = pl.ds(pl.multiple_of(j * size, size), size)
        return [
            pltpu.make_async_copy(
                ref.at[pl.ds(place, size), :], out.at[slot, pl.ds(k * size, size)], sems.at[i, j, k]
            )
            for k, ref in enumerate((own, other))
        ]

    outs = tuple(enumerate((b0, b1, b2, b3)))
    for i, out in outs:

        def start(j, carry, i=i, out=out):
            for copy in copies(out, i, j):
                copy.start()
            return carry

        lax.fori_loop(0, 4, start, 0)
    for i, out in outs:

        def wait(j, carry, i=i, out=out):
            for copy in copies(out, i, j):
                copy.wait()
            return carry

        lax.fori_loop(0, 4, wait, 0)


def left_body(pos, dep, b0, b1, b2, b3, p0, p1, top, low, p3, keep, send):
    size = keep.shape[1]
    total = None
    for basis, piece in ((b0, p0[...]), (b1, p1[...]), (b3, p3[...]), (b2, None)):
        if piece is None:
            piece = jnp.concatenate([top[...], low[...]], 0)
        part = dot(piece, basis[...])
        total = part if total is None else total + part
    keep[...] = total[:, :size].astype(bf16)
    send[...] = total[:, size:].astype(bf16)


def left_tokens_body(
    pos, dep_a, dep_b, b0, b1, b2, b3, gain, p0, p1, top, low, p3, keep, send, turned, first, square
):
    cols = size = send.shape[1]
    parts = (b0, b1, b2, b3)
    n_tok = p0.shape[0] - cols
    squares = 0.0
    total = None
    for i, piece in ((0, p0[...]), (1, p1[...]), (3, p3[...]), (2, None)):
        if piece is None:
            piece = jnp.concatenate([top[...], low[...]], 0)
        gains = jnp.concatenate([gain[chip_place(pos, i, j) * 2 + pos[C]] for j in range(4)], -1)
        feats = piece[cols:, :].astype(f32)
        squares = squares + jnp.sum(feats * feats, -1, keepdims=True)
        feats = feats * gains * token_unit
        if i == 0:
            first[...] = feats[:, :size].reshape(first.shape)
        piece = jnp.concatenate([piece[:cols, :], feats.astype(bf16)], 0)
        part = dot(piece, parts[i][...])
        total = part if total is None else total + part
    keep[:cols, :] = total[:cols, :size]
    send[:cols, :] = total[:cols, size:]
    for k in range(2):
        turned[k] = total[cols:, k * size : (k + 1) * size].reshape(2, n_tok // 2, size)
    square[...] = jnp.broadcast_to(squares, (n_tok, size)).reshape(square.shape)
    rows = n_tok // 2
    core = pos[C]
    for out, which, order in ((keep, core, (1, 0)), (send, 1 - core, (0, 1))):
        at = cols
        for value in (turned[order[0], which], turned[order[1], which], first[which], square[which]):
            out[at : at + rows, :] = value
            at += rows


def pair_body(pos, keep, core, low, both, out):
    out[0] = (keep[...].astype(f32) + core[...].astype(f32)).T.astype(bf16)
    out[1] = (low[...].astype(f32) + both[...].astype(f32)).T.astype(bf16)


def left_tokens_sum_body(pos, keep, recv, all_out, out):
    cols = keep.shape[1]
    rows = (out.shape[0] - cols) // 4
    out[:cols, :] = (keep[:cols, :] + recv[:cols, :]).T.astype(bf16)
    parts = [slice(cols + k * rows, cols + (k + 1) * rows) for k in range(4)]
    square = keep[parts[3], :] + recv[parts[3], :]
    scale = lax.rsqrt(square / (32 * cols) + norm_eps) * (1.0 / token_unit)
    turned_other = keep[parts[0], :] + recv[parts[0], :]
    turned_own = keep[parts[1], :] + recv[parts[1], :]
    values = (
        keep[parts[2], :] * scale,
        recv[parts[2], :] * scale,
        turned_own * scale * (-learn_rate),
        turned_other * scale * (-learn_rate),
    )
    for part, value in zip(parts, values):
        out[part, :] = value.astype(bf16)
    for n in range(8):
        all_out[n] = out[...]


def new_variance(pos, right, variance, s0, s1, s2, s3):
    cols = right.shape[1]
    rot = None
    for j, piece in enumerate((s0, s1, s2, s3)):
        for i in range(2):
            place = ((pos[L] + 2 - i) % 2) * 4 + (pos[Y] + 4 - j) % 4
            rows = pl.ds(pl.multiple_of(place * cols, cols), cols)
            part = dot(piece[i], right[rows, :])
            rot = part if rot is None else rot + part
    return beta_two * variance[...] + (1.0 - beta_two) * rot * rot


def direction_body(pos, right, variance, s0, s1, s2, s3, left, variance_new, out):
    cols = right.shape[1]
    variance_new[...] = new_variance(pos, right, variance, s0, s1, s2, s3)
    rot = None
    for n in range(8):
        part = dot(left[n, :cols, :], right[n * cols : (n + 1) * cols, :])
        rot = part if rot is None else rot + part
    corr_one = 1.0 - beta_one**adam_step
    corr_two = 1.0 - beta_two**adam_step
    value = rot / corr_one / (jnp.sqrt(variance_new[...] / corr_two) + adam_eps)
    value = value.astype(bf16)
    for n in range(8):
        out[n] = dot(value, right[n * cols : (n + 1) * cols, :], 1, 1).astype(bf16)


def back_body(pos, parts, out):
    out[...] = sum(parts[n].astype(f32) for n in range(8)).astype(bf16)


def update_far_body(pos, back_own, back_other, kv, basis, top, low, whole):
    update_body((2,), pos, back_own, back_other, kv, basis, whole)
    half = top.shape[0]
    top[...] = whole[:half, :]
    low[...] = whole[half:, :]


def add_halves_body(pos, one, three, top, low, o1, o3):
    half = top.shape[0]
    o1[:half, :] = (one[:half, :].astype(f32) + top[...].astype(f32)).astype(bf16)
    o1[half:, :] = one[half:, :]
    o3[:half, :] = three[:half, :]
    o3[half:, :] = (three[half:, :].astype(f32) + low[...].astype(f32)).astype(bf16)


def update_body(steps, pos, back_own, back_other, kv, *refs):
    size = back_own.shape[0]
    rows = kv.shape[2]
    back = jnp.concatenate([back_own[...], back_other[...]], 0)
    many = len(steps)
    for i, basis, out in zip(steps, refs[:many], refs[many:]):
        for n in range(0, 4, 2):
            part = slice(n * size, (n + 2) * size)
            out[part, :] = dot(basis[part, :], back).astype(bf16)
        for j in range(4):
            out[4 * size + j * rows : 4 * size + (j + 1) * rows, :] = kv[i, j]


def kv_body(pos, w_own, w_other, b_own, b_other, left, total):
    size = w_own.shape[0]
    many = (left.shape[1] - size) // 4
    rows = many // 2
    value = None
    for k, ref in enumerate((w_own, w_other, b_own, b_other)):
        part = slice(size + k * many, size + (k + 1) * many)
        part = dot(jnp.concatenate([left[n, part, :] for n in range(8)], 0), ref[...])
        value = part if value is None else value + part
    for n in range(8):
        step_x = (pos[X] + 4 - n % 4) % 4
        for low in range(2):
            step_z = (pos[Z] + 4 - (n // 4) * 2 - low) % 4
            first = (2 * n + low) * rows
            total[step_x, step_z] = value[first : first + rows].astype(bf16)


def sums_body(pos, a, b, c, keep, o1, o2, o3):
    rows = o1.shape[0] - o1.shape[1]
    size = o1.shape[0] - rows
    refs = (a, b, c)
    for j, out in enumerate((keep, o1, o2, o3)):
        for to, at, many in ((0, j * size, size), (size, 4 * size + j * rows, rows)):
            total = sum(ref[at : at + many, :].astype(f32) for ref in refs)
            out[to : to + many, :] = total.astype(out.dtype)


def attend_old_body(pos, dep, query, keys, values, out, row_max, row_sum):
    seqs, rows, head_dim = query.shape
    scaling = float(head_dim) ** (-0.5)
    cells = lax.broadcasted_iota(jnp.int32, (rows, keys.shape[1]), 1)
    for s in range(seqs):
        score = dot(query[s], keys[s], 1, 1) * scaling
        inside = cells < pos[len(AXES) + s]
        score = jnp.where(inside, score, -1e30)
        top = jnp.max(score, -1, keepdims=True)
        value = jnp.where(inside, jnp.exp(score - top), 0.0)
        out[s] = dot(value.astype(bf16), values[s])
        row_max[s] = jnp.broadcast_to(top, (rows, head_dim))
        row_sum[s] = jnp.broadcast_to(jnp.sum(value, -1, keepdims=True), (rows, head_dim))


def finish_body(
    pos, kept, one, two, three, cosine, sine_part, query, old, row_max, row_sum, update, out, stage
):
    size = update.shape[0]
    total = kept[...] + sum(ref[...].astype(f32) for ref in (one, two, three))
    update[...] = total[:size]
    total = total[size:]
    steps = out.shape[1]
    seqs, rows, head_dim = query.shape
    scaling = float(head_dim) ** (-0.5)
    count = total.shape[0]
    keys = total[:, :head_dim]
    values = total[:, head_dim:].astype(bf16)
    half = head_dim // 2
    turned = jnp.concatenate([keys[:, half:], keys[:, :half]], 1)
    keys = (keys * cosine[...] + turned * sine_part[...]).astype(bf16)
    cells = lax.broadcasted_iota(jnp.int32, (rows, count), 1)
    row_ids = lax.broadcasted_iota(jnp.int32, (rows, count), 0)
    query_step = sum((row_ids >= t * (rows // steps)).astype(jnp.int32) for t in range(1, steps))
    for s in range(seqs):
        score = dot(query[s], keys, 1, 1) * scaling
        inside = (cells >= s * steps) & (cells <= s * steps + query_step)
        score = jnp.where(inside, score, -1e30)
        top = row_max[s]
        new_top = jnp.maximum(top, jnp.max(score, -1, keepdims=True))
        shrink = jnp.exp(top - new_top)
        value = jnp.where(inside, jnp.exp(score - new_top[:, :1]), 0.0)
        sums = row_sum[s] * shrink + jnp.sum(value, -1, keepdims=True)
        stage[...] = (old[s] * shrink + dot(value.astype(bf16), values)) / sums
        group = rows // steps
        for g in range(group):
            out[s, :, g * head_dim : (g + 1) * head_dim] = stage[g::group, :]


def exchange(array):
    return lax.all_to_all(array, ("zl", "y"), 0, 0, tiled=True)


def ring_first(array):
    return shift(array, "x", 1), shift(array, "x", -1)


def ring_gather(array, first, dep):
    one, three = first
    half = array.shape[0] // 2
    top, low = after(one, dep[0])[:half], after(three, dep[-1])[half:]
    return [array, one, shift(top, "x", 1), shift(low, "x", -1), three]


def after(array, *deps):
    return lax.optimization_barrier((array,) + deps)[0]


def shards(
    master,
    grad,
    moment,
    variance,
    q_left,
    q_right,
    embed,
    gain,
    token_ids,
    queries,
    k_cache,
    v_cache,
    cache_len,
):
    axis_places = jnp.stack([lax.axis_index(name) for name in AXES]).astype(jnp.int32)
    position = jnp.concatenate([axis_places, cache_len])
    group_at = lax.axis_index(("zl", "y"))
    rows, cols = grad.shape
    square = (rows, cols)

    grad_t = pl.pallas_call(
        turn_body,
        out_shape=jax.ShapeDtypeStruct((cols, rows), bf16),
        compiler_params=pltpu.CompilerParams(vmem_limit_bytes=VMEM_BYTES),
    )(grad)
    grad_z = others(grad_t, "zh")

    flat_ids = token_ids.reshape(4, 2, 2, 2, -1)
    tok_rows = flat_ids.shape[-1]
    flat_ids = after(jnp.transpose(flat_ids, (1, 0, 3, 2, 4)).reshape(-1), grad_z[0])
    n_tok = flat_ids.shape[0]
    vocab_rows = embed.shape[0]
    local_ids = jnp.clip(flat_ids - group_at * vocab_rows, 0, vocab_rows - 1)
    picked = embed.at[local_ids].get(mode="promise_in_bounds").reshape(8, n_tok // 8, rows)
    arrived = exchange(picked)
    owner = (flat_ids // vocab_rows).reshape(8, n_tok // 8)
    owner = lax.dynamic_index_in_dim(owner, group_at, 0, keepdims=False).reshape(-1, 1)

    q_other = swap(after(q_left, grad_t))
    basis = call(
        basis_body,
        [((4 * rows, 2 * rows), bf16)] * 4,
        position,
        far=(q_left, q_other),
        scratch=[pltpu.SemaphoreType.DMA((4, 4, 2))],
    )
    moment_new, moment_t, master_low = call(
        moment_body,
        [(square, f32), ((cols, rows), bf16), (square, bf16)],
        position,
        after(grad, grad_t),
        moment,
        master,
    )
    deep = cols + n_tok // 8
    (grad_x,) = call(wide_body, [((cols, 4 * rows), bf16)], position, grad_t, *grad_z, deps=(picked, q_other))
    grad_first = ring_first(grad_x)
    (moment_z,) = call(
        moment_tokens_body,
        [((deep, rows), bf16)],
        position,
        moment_t,
        arrived,
        owner,
    )
    moment_z = after(moment_z, grad_x)
    grad_pieces = ring_gather(grad_x, grad_first, [moment_z])
    moment_others = others(moment_z, "zh")
    (moment_x,) = call(
        wide_body, [((deep, 4 * rows), bf16)], position, moment_z, *moment_others, deps=(*grad_pieces[2:4], basis[0])
    )
    moment_first = ring_first(moment_x)

    master_other = swap(master_low)

    seqs, steps = queries.shape[0], queries.shape[1]
    head_dim = k_cache.shape[-1]
    query_rows = queries.reshape(seqs, -1, head_dim)
    old_out, old_max, old_sum = call(
        attend_old_body,
        [(query_rows.shape, f32)] * 3,
        position,
        query_rows,
        k_cache.reshape(seqs, -1, head_dim),
        v_cache.reshape(seqs, -1, head_dim),
        deps=(moment_others[0],),
    )
    token_at = (cache_len[:, None] + jnp.arange(steps, dtype=jnp.int32)[None, :]).reshape(-1, 1)
    inverse = rope_base ** (-(jnp.arange(head_dim // 2, dtype=f32) * 2.0 / head_dim))
    angles = after(token_at, moment_others[0]).astype(f32) * inverse
    cosine = jnp.concatenate([jnp.cos(angles)] * 2, 1)
    sine_part = jnp.concatenate([-jnp.sin(angles), jnp.sin(angles)], 1)

    keep, send = call(
        left_body,
        [((cols, rows), bf16)] * 2,
        position,
        *basis,
        *grad_pieces,
        deps=(moment_x,),
    )
    (left_g,) = call(
        pair_body,
        [((2,) + square, bf16)],
        position,
        keep,
        swap(send),
        shift(keep, "zl", 1),
        lax.ppermute(send, ("c", "zl"), [(i, 3 - i) for i in range(4)]),
    )
    left_others = others(left_g, "y")
    moment_pieces = ring_gather(moment_x, moment_first, left_others[::2])
    keep, send = call(
        left_tokens_body,
        [((cols + n_tok // 4, rows), f32)] * 2,
        position,
        *basis,
        gain.reshape(32, 1, rows),
        *moment_pieces,
        deps=(left_others[1], master_other),
        scratch=[
            pltpu.VMEM((2, 2, n_tok // 16, rows), f32),
            pltpu.VMEM((2, n_tok // 16, rows), f32),
            pltpu.VMEM((2, n_tok // 16, rows), f32),
        ],
    )
    (left_m,) = call(
        left_tokens_sum_body,
        [((8, cols + n_tok // 4, rows), bf16)],
        position,
        keep,
        swap(send),
        scratch=[pltpu.VMEM((cols + n_tok // 4, rows), bf16)],
    )
    left_m = exchange(left_m)

    variance_new, parts = call(
        direction_body,
        [(square, f32), ((8,) + square, bf16)],
        position,
        q_right,
        variance,
        left_g,
        *left_others,
        left_m,
    )
    (back_own,) = call(back_body, [(square, bf16)], position, exchange(parts))
    back_other = swap(back_own)

    (kv,) = call(
        kv_body,
        [((4, 4, tok_rows, cols), bf16)],
        position,
        master_low,
        master_other,
        back_own,
        back_other,
        left_m,
    )

    many = 4 * (rows + tok_rows)
    top, low = call(
        update_far_body,
        [((many // 2, cols), bf16)] * 2,
        position,
        back_own,
        back_other,
        kv,
        basis[2],
        scratch=[pltpu.VMEM((many, cols), bf16)],
    )
    top, low = shift(top, "x", -1), shift(low, "x", 1)
    one, three, zero = call(
        functools.partial(update_body, (1, 3, 0)),
        [((many, cols), bf16)] * 3,
        position,
        back_own,
        back_other,
        kv,
        basis[1],
        basis[3],
        basis[0],
    )
    one, three = call(
        add_halves_body, [((many, cols), bf16)] * 2, position, one, three, top, low
    )
    parts = call(
        sums_body,
        [((rows + tok_rows, cols), f32)] + [((rows + tok_rows, cols), bf16)] * 3,
        position,
        zero,
        shift(one, "x", -1),
        shift(three, "x", 1),
    )
    update, attended = call(
        finish_body,
        [(square, f32), (queries.shape, f32)],
        position,
        parts[0],
        *scatter(parts, "zh"),
        cosine,
        sine_part,
        query_rows,
        old_out,
        old_max,
        old_sum,
        scratch=[pltpu.VMEM(query_rows.shape[1:], f32)],
    )
    return (update, moment_new, variance_new, attended)


def solution(mesh):
    fine = Mesh(mesh.devices.reshape([SIZES[name] for name in AXES]), AXES)
    fsdp = ("x", "zh", "c")
    tp = ("zl", "y")
    in_specs = (
        P(fsdp, tp),
        P(fsdp, tp),
        P(fsdp, tp),
        P(fsdp, tp),
        P(None, fsdp),
        P(None, tp),
        P(tp, fsdp),
        P(),
        P(),
        P(fsdp, None, tp),
        P(fsdp, tp, None, None),
        P(fsdp, tp, None, None),
        P(fsdp),
    )
    out_specs = (P(fsdp, tp), P(fsdp, tp), P(fsdp, tp), P(fsdp, None, tp))
    return jax.shard_map(shards, mesh=fine, in_specs=in_specs, out_specs=out_specs, check_vma=False)
```

```python
import functools

import jax
import jax.numpy as jnp
from jax import lax
from jax.experimental import pallas as pl
from jax.experimental.pallas import tpu as pltpu
from jax.sharding import Mesh, PartitionSpec as P

beta_one = 0.9
beta_two = 0.95
adam_eps = 1e-08
learn_rate = 0.003
adam_step = 20
norm_eps = 1e-06
rope_base = 1000000.0
token_unit = 2.0**-10

AXES = ("x", "zh", "c", "zl", "y")
SIZES = {"x": 4, "zh": 4, "c": 2, "zl": 2, "y": 4}
X, Z, C, L, Y = range(5)
f32 = jnp.float32
bf16 = jnp.bfloat16
VMEM_BYTES = 20 * 1024 * 1024


def call(body, outs, position, *args, far=(), deps=(), scratch=(), space=pltpu.VMEM):
    vmem = pl.BlockSpec(memory_space=pltpu.VMEM)
    return pl.pallas_call(
        body,
        out_shape=[jax.ShapeDtypeStruct(shape, kind) for shape, kind in outs],
        in_specs=[pl.BlockSpec(memory_space=pltpu.SMEM)]
        + [pl.BlockSpec(memory_space=pltpu.HBM)] * len(far)
        + [pl.BlockSpec(memory_space=pl.ANY)] * len(deps)
        + [vmem] * len(args),
        out_specs=[pl.BlockSpec(memory_space=space)] * len(outs),
        scratch_shapes=list(scratch),
        compiler_params=pltpu.CompilerParams(vmem_limit_bytes=VMEM_BYTES),
    )(position, *far, *deps, *args)


def shift(array, axis, by):
    size = SIZES[axis]
    return lax.ppermute(array, axis, [(i, (i + by) % size) for i in range(size)])


def swap(array):
    return shift(array, "c", 1)


def others(array, axis):
    return [shift(array, axis, k) for k in range(1, SIZES[axis])]


def scatter(arrays, axis):
    return [shift(array, axis, -k) for k, array in enumerate(arrays) if k]


def dot(left, right, left_dim=1, right_dim=0):
    return lax.dot_general(
        left, right, (((left_dim,), (right_dim,)), ((), ())), preferred_element_type=f32
    )


def chip_place(pos, i, j):
    return ((pos[X] + 4 - i) % 4) * 4 + (pos[Z] + 4 - j) % 4


def turn_body(array, out):
    out[...] = array[...].astype(f32).T.astype(bf16)


def moment_body(pos, grad, moment, master, moment_new, turned, low):
    new = beta_one * moment[...] + (1.0 - beta_one) * grad[...].astype(f32)
    moment_new[...] = new
    turned[...] = new.astype(bf16).astype(f32).T.astype(bf16)
    low[...] = master[...].astype(bf16)


def moment_tokens_body(pos, turned, arrived, owner, out):
    cols = turned.shape[0]
    out[:cols, :] = turned[...]
    total = None
    for i in range(8):
        part = jnp.where(owner[...] == i, arrived[i].astype(f32), 0.0)
        total = part if total is None else total + part
    out[cols:, :] = total.astype(bf16)


def wide_body(pos, *refs):
    out = refs[-1]
    for i, piece in enumerate(refs[-5:-1]):
        out[:, i * piece.shape[1] : (i + 1) * piece.shape[1]] = piece[...]


def basis_body(pos, own, other, b0, b1, b2, b3, sems):
    size = b0.shape[1] // 2

    def copies(out, i, j):
        place = pl.multiple_of((chip_place(pos, i, j) * 2 + pos[C]) * size, size)
        slot = pl.ds(pl.multiple_of(j * size, size), size)
        return [
            pltpu.make_async_copy(
                ref.at[pl.ds(place, size), :], out.at[slot, pl.ds(k * size, size)], sems.at[i, j, k]
            )
            for k, ref in enumerate((own, other))
        ]

    outs = tuple(enumerate((b0, b1, b2, b3)))
    for i, out in outs:

        def start(j, carry, i=i, out=out):
            for copy in copies(out, i, j):
                copy.start()
            return carry

        lax.fori_loop(0, 4, start, 0)
    for i, out in outs:

        def wait(j, carry, i=i, out=out):
            for copy in copies(out, i, j):
                copy.wait()
            return carry

        lax.fori_loop(0, 4, wait, 0)


def left_body(pos, dep, b0, b1, b2, b3, p0, p1, top, low, p3, keep, send):
    size = keep.shape[1]
    total = None
    for basis, piece in ((b0, p0[...]), (b1, p1[...]), (b3, p3[...]), (b2, None)):
        if piece is None:
            piece = jnp.concatenate([top[...], low[...]], 0)
        part = dot(piece, basis[...])
        total = part if total is None else total + part
    keep[...] = total[:, :size].astype(bf16)
    send[...] = total[:, size:].astype(bf16)


def left_tokens_body(
    pos, dep_a, dep_b, b0, b1, b2, b3, gain, p0, p1, top, low, p3, keep, send, turned, first, square
):
    cols = size = send.shape[1]
    parts = (b0, b1, b2, b3)
    n_tok = p0.shape[0] - cols
    squares = 0.0
    total = None
    for i, piece in ((0, p0[...]), (1, p1[...]), (3, p3[...]), (2, None)):
        if piece is None:
            piece = jnp.concatenate([top[...], low[...]], 0)
        gains = jnp.concatenate([gain[chip_place(pos, i, j) * 2 + pos[C]] for j in range(4)], -1)
        feats = piece[cols:, :].astype(f32)
        squares = squares + jnp.sum(feats * feats, -1, keepdims=True)
        feats = feats * gains * token_unit
        if i == 0:
            first[...] = feats[:, :size].reshape(first.shape)
        piece = jnp.concatenate([piece[:cols, :], feats.astype(bf16)], 0)
        part = dot(piece, parts[i][...])
        total = part if total is None else total + part
    keep[:cols, :] = total[:cols, :size]
    send[:cols, :] = total[:cols, size:]
    for k in range(2):
        turned[k] = total[cols:, k * size : (k + 1) * size].reshape(2, n_tok // 2, size)
    square[...] = jnp.broadcast_to(squares, (n_tok, size)).reshape(square.shape)
    rows = n_tok // 2
    core = pos[C]
    for out, which, order in ((keep, core, (1, 0)), (send, 1 - core, (0, 1))):
        at = cols
        for value in (turned[order[0], which], turned[order[1], which], first[which], square[which]):
            out[at : at + rows, :] = value
            at += rows


def pair_body(pos, keep, core, low, both, out):
    out[0] = (keep[...].astype(f32) + core[...].astype(f32)).T.astype(bf16)
    out[1] = (low[...].astype(f32) + both[...].astype(f32)).T.astype(bf16)


def left_tokens_sum_body(pos, keep, recv, all_out, out):
    cols = keep.shape[1]
    rows = (out.shape[0] - cols) // 4
    out[:cols, :] = (keep[:cols, :] + recv[:cols, :]).T.astype(bf16)
    parts = [slice(cols + k * rows, cols + (k + 1) * rows) for k in range(4)]
    square = keep[parts[3], :] + recv[parts[3], :]
    scale = lax.rsqrt(square / (32 * cols) + norm_eps) * (1.0 / token_unit)
    turned_other = keep[parts[0], :] + recv[parts[0], :]
    turned_own = keep[parts[1], :] + recv[parts[1], :]
    values = (
        keep[parts[2], :] * scale,
        recv[parts[2], :] * scale,
        turned_own * scale * (-learn_rate),
        turned_other * scale * (-learn_rate),
    )
    for part, value in zip(parts, values):
        out[part, :] = value.astype(bf16)
    for n in range(8):
        all_out[n] = out[...]


def new_variance(pos, right, variance, s0, s1, s2, s3):
    cols = right.shape[1]
    rot = None
    for j, piece in enumerate((s0, s1, s2, s3)):
        for i in range(2):
            place = ((pos[L] + 2 - i) % 2) * 4 + (pos[Y] + 4 - j) % 4
            rows = pl.ds(pl.multiple_of(place * cols, cols), cols)
            part = dot(piece[i], right[rows, :])
            rot = part if rot is None else rot + part
    return beta_two * variance[...] + (1.0 - beta_two) * rot * rot


def direction_body(pos, right, variance, s0, s1, s2, s3, left, variance_new, out):
    cols = right.shape[1]
    variance_new[...] = new_variance(pos, right, variance, s0, s1, s2, s3)
    rot = None
    for n in range(8):
        part = dot(left[n, :cols, :], right[n * cols : (n + 1) * cols, :])
        rot = part if rot is None else rot + part
    corr_one = 1.0 - beta_one**adam_step
    corr_two = 1.0 - beta_two**adam_step
    value = rot / corr_one / (jnp.sqrt(variance_new[...] / corr_two) + adam_eps)
    value = value.astype(bf16)
    for n in range(8):
        out[n] = dot(value, right[n * cols : (n + 1) * cols, :], 1, 1).astype(bf16)


def back_body(pos, parts, out):
    out[...] = sum(parts[n].astype(f32) for n in range(8)).astype(bf16)


def update_far_body(
    pos, w_own, w_other, b_own, b_other, side, basis, top, low, kv, whole
):
    kv_body(pos, w_own, w_other, b_own, b_other, side, kv)
    update_body((2,), pos, b_own, b_other, kv, basis, whole)
    half = top.shape[0]
    top[...] = whole[:half, :]
    low[...] = whole[half:, :]


def add_halves_body(pos, one, three, top, low, o1, o3):
    half = top.shape[0]
    o1[:half, :] = one[:half, :] + top[...]
    o1[half:, :] = one[half:, :]
    o3[:half, :] = three[:half, :]
    o3[half:, :] = three[half:, :] + low[...]


def update_body(steps, pos, back_own, back_other, kv, *refs):
    size = back_own.shape[0]
    rows = kv.shape[2]
    back = jnp.concatenate([back_own[...], back_other[...]], 0)
    many = len(steps)
    for i, basis, out in zip(steps, refs[:many], refs[many:]):
        for n in range(0, 4, 2):
            part = slice(n * size, (n + 2) * size)
            out[part, :] = dot(basis[part, :], back).astype(bf16)
        for j in range(4):
            out[4 * size + j * rows : 4 * size + (j + 1) * rows, :] = kv[i, j]


def kv_body(pos, w_own, w_other, b_own, b_other, left, total):
    size = w_own.shape[0]
    many = (left.shape[1] - size) // 4
    rows = many // 2
    value = None
    for k, ref in enumerate((w_own, w_other, b_own, b_other)):
        part = slice(size + k * many, size + (k + 1) * many)
        part = dot(jnp.concatenate([left[n, part, :] for n in range(8)], 0), ref[...])
        value = part if value is None else value + part
    for n in range(8):
        step_x = (pos[X] + 4 - n % 4) % 4
        for low in range(2):
            step_z = (pos[Z] + 4 - (n // 4) * 2 - low) % 4
            first = (2 * n + low) * rows
            total[step_x, step_z] = value[first : first + rows].astype(bf16)


def sums_body(pos, a, b, c, keep, o1, o2, o3):
    rows = o1.shape[0] - o1.shape[1]
    size = o1.shape[0] - rows
    refs = (a, b, c)
    for j, out in enumerate((keep, o1, o2, o3)):
        for to, at, many in ((0, j * size, size), (size, 4 * size + j * rows, rows)):
            total = sum(ref[at : at + many, :].astype(f32) for ref in refs)
            out[to : to + many, :] = total.astype(out.dtype)


def attend_old_body(pos, dep, query, keys, values, out, row_max, row_sum):
    seqs, rows, head_dim = query.shape
    scaling = float(head_dim) ** (-0.5)
    cells = lax.broadcasted_iota(jnp.int32, (rows, keys.shape[1]), 1)
    for s in range(seqs):
        score = dot(query[s], keys[s], 1, 1) * scaling
        inside = cells < pos[len(AXES) + s]
        score = jnp.where(inside, score, -1e30)
        top = jnp.max(score, -1, keepdims=True)
        value = jnp.where(inside, jnp.exp(score - top), 0.0)
        out[s] = dot(value.astype(bf16), values[s])
        row_max[s] = jnp.broadcast_to(top, (rows, head_dim))
        row_sum[s] = jnp.broadcast_to(jnp.sum(value, -1, keepdims=True), (rows, head_dim))


def finish_body(
    pos, kept, one, two, three, cosine, sine_part, query, old, row_max, row_sum, update, out, stage
):
    size = update.shape[0]
    total = kept[...] + sum(ref[...].astype(f32) for ref in (one, two, three))
    update[...] = total[:size]
    total = total[size:]
    steps = out.shape[1]
    seqs, rows, head_dim = query.shape
    scaling = float(head_dim) ** (-0.5)
    count = total.shape[0]
    keys = total[:, :head_dim]
    values = total[:, head_dim:].astype(bf16)
    half = head_dim // 2
    turned = jnp.concatenate([keys[:, half:], keys[:, :half]], 1)
    keys = (keys * cosine[...] + turned * sine_part[...]).astype(bf16)
    cells = lax.broadcasted_iota(jnp.int32, (rows, count), 1)
    row_ids = lax.broadcasted_iota(jnp.int32, (rows, count), 0)
    query_step = sum((row_ids >= t * (rows // steps)).astype(jnp.int32) for t in range(1, steps))
    for s in range(seqs):
        score = dot(query[s], keys, 1, 1) * scaling
        inside = (cells >= s * steps) & (cells <= s * steps + query_step)
        score = jnp.where(inside, score, -1e30)
        top = row_max[s]
        new_top = jnp.maximum(top, jnp.max(score, -1, keepdims=True))
        shrink = jnp.exp(top - new_top)
        value = jnp.where(inside, jnp.exp(score - new_top[:, :1]), 0.0)
        sums = row_sum[s] * shrink + jnp.sum(value, -1, keepdims=True)
        stage[...] = (old[s] * shrink + dot(value.astype(bf16), values)) / sums
        group = rows // steps
        for g in range(group):
            out[s, :, g * head_dim : (g + 1) * head_dim] = stage[g::group, :]


def exchange(array):
    return lax.all_to_all(array, ("zl", "y"), 0, 0, tiled=True)


def ring_first(array):
    return shift(array, "x", 1), shift(array, "x", -1)


def ring_gather(array, first, dep):
    one, three = first
    half = array.shape[0] // 2
    top, low = after(one, dep[0])[:half], after(three, dep[-1])[half:]
    return [array, one, shift(top, "x", 1), shift(low, "x", -1), three]


def after(array, *deps):
    return lax.optimization_barrier((array,) + deps)[0]


def shards(
    master,
    grad,
    moment,
    variance,
    q_left,
    q_right,
    embed,
    gain,
    token_ids,
    queries,
    k_cache,
    v_cache,
    cache_len,
):
    axis_places = jnp.stack([lax.axis_index(name) for name in AXES]).astype(jnp.int32)
    position = jnp.concatenate([axis_places, cache_len])
    group_at = lax.axis_index(("zl", "y"))
    rows, cols = grad.shape
    square = (rows, cols)

    grad_t = pl.pallas_call(
        turn_body,
        out_shape=jax.ShapeDtypeStruct((cols, rows), bf16),
        compiler_params=pltpu.CompilerParams(vmem_limit_bytes=VMEM_BYTES),
    )(grad)
    grad_z = others(grad_t, "zh")

    flat_ids = token_ids.reshape(4, 2, 2, 2, -1)
    tok_rows = flat_ids.shape[-1]
    flat_ids = after(jnp.transpose(flat_ids, (1, 0, 3, 2, 4)).reshape(-1), grad_z[0])
    n_tok = flat_ids.shape[0]
    vocab_rows = embed.shape[0]
    local_ids = jnp.clip(flat_ids - group_at * vocab_rows, 0, vocab_rows - 1)
    picked = embed.at[local_ids].get(mode="promise_in_bounds").reshape(8, n_tok // 8, rows)
    arrived = exchange(picked)
    owner = (flat_ids // vocab_rows).reshape(8, n_tok // 8)
    owner = lax.dynamic_index_in_dim(owner, group_at, 0, keepdims=False).reshape(-1, 1)

    q_other = swap(after(q_left, grad_t))
    basis = call(
        basis_body,
        [((4 * rows, 2 * rows), bf16)] * 4,
        position,
        far=(q_left, q_other),
        scratch=[pltpu.SemaphoreType.DMA((4, 4, 2))],
    )
    moment_new, moment_t, master_low = call(
        moment_body,
        [(square, f32), ((cols, rows), bf16), (square, bf16)],
        position,
        after(grad, grad_t),
        moment,
        master,
    )
    deep = cols + n_tok // 8
    (grad_x,) = call(wide_body, [((cols, 4 * rows), bf16)], position, grad_t, *grad_z, deps=(picked, q_other))
    grad_first = ring_first(grad_x)
    (moment_z,) = call(
        moment_tokens_body,
        [((deep, rows), bf16)],
        position,
        moment_t,
        arrived,
        owner,
    )
    moment_z = after(moment_z, grad_x)
    grad_pieces = ring_gather(grad_x, grad_first, [moment_z])
    moment_others = others(moment_z, "zh")
    (moment_x,) = call(
        wide_body, [((deep, 4 * rows), bf16)], position, moment_z, *moment_others, deps=(*grad_pieces[2:4], basis[0])
    )
    moment_first = ring_first(moment_x)

    master_other = swap(master_low)

    seqs, steps = queries.shape[0], queries.shape[1]
    head_dim = k_cache.shape[-1]
    query_rows = queries.reshape(seqs, -1, head_dim)
    old_out, old_max, old_sum = call(
        attend_old_body,
        [(query_rows.shape, f32)] * 3,
        position,
        query_rows,
        k_cache.reshape(seqs, -1, head_dim),
        v_cache.reshape(seqs, -1, head_dim),
        deps=(moment_others[0],),
    )
    token_at = (cache_len[:, None] + jnp.arange(steps, dtype=jnp.int32)[None, :]).reshape(-1, 1)
    inverse = rope_base ** (-(jnp.arange(head_dim // 2, dtype=f32) * 2.0 / head_dim))
    angles = after(token_at, moment_others[0]).astype(f32) * inverse
    cosine = jnp.concatenate([jnp.cos(angles)] * 2, 1)
    sine_part = jnp.concatenate([-jnp.sin(angles), jnp.sin(angles)], 1)

    keep, send = call(
        left_body,
        [((cols, rows), bf16)] * 2,
        position,
        *basis,
        *grad_pieces,
        deps=(moment_x,),
    )
    (left_g,) = call(
        pair_body,
        [((2,) + square, bf16)],
        position,
        keep,
        swap(send),
        shift(keep, "zl", 1),
        lax.ppermute(send, ("c", "zl"), [(i, 3 - i) for i in range(4)]),
    )
    left_others = others(left_g, "y")
    moment_pieces = ring_gather(moment_x, moment_first, left_others[::2])
    keep, send = call(
        left_tokens_body,
        [((cols + n_tok // 4, rows), f32)] * 2,
        position,
        *basis,
        gain.reshape(32, 1, rows),
        *moment_pieces,
        deps=(left_others[1], master_other),
        scratch=[
            pltpu.VMEM((2, 2, n_tok // 16, rows), f32),
            pltpu.VMEM((2, n_tok // 16, rows), f32),
            pltpu.VMEM((2, n_tok // 16, rows), f32),
        ],
    )
    (left_m,) = call(
        left_tokens_sum_body,
        [((8, cols + n_tok // 4, rows), bf16)],
        position,
        keep,
        swap(send),
        scratch=[pltpu.VMEM((cols + n_tok // 4, rows), bf16)],
    )
    left_m = exchange(left_m)

    variance_new, parts = call(
        direction_body,
        [(square, f32), ((8,) + square, bf16)],
        position,
        q_right,
        variance,
        left_g,
        *left_others,
        left_m,
    )
    (back_own,) = call(back_body, [(square, bf16)], position, exchange(parts))
    back_other = swap(back_own)

    many = 4 * (rows + tok_rows)
    top, low, kv = call(
        update_far_body,
        [((many // 2, cols), bf16)] * 2 + [((4, 4, tok_rows, cols), bf16)],
        position,
        master_low,
        master_other,
        back_own,
        back_other,
        left_m,
        basis[2],
        scratch=[pltpu.VMEM((many, cols), bf16)],
    )
    top, low = shift(top, "x", -1), shift(low, "x", 1)
    one, three, zero = call(
        functools.partial(update_body, (1, 3, 0)),
        [((many, cols), bf16)] * 3,
        position,
        back_own,
        back_other,
        kv,
        basis[1],
        basis[3],
        basis[0],
    )
    one, three = call(
        add_halves_body, [((many, cols), bf16)] * 2, position, one, three, top, low
    )
    parts = call(
        sums_body,
        [((rows + tok_rows, cols), f32)] + [((rows + tok_rows, cols), bf16)] * 3,
        position,
        zero,
        shift(one, "x", -1),
        shift(three, "x", 1),
    )
    update, attended = call(
        finish_body,
        [(square, f32), (queries.shape, f32)],
        position,
        parts[0],
        *scatter(parts, "zh"),
        cosine,
        sine_part,
        query_rows,
        old_out,
        old_max,
        old_sum,
        scratch=[pltpu.VMEM(query_rows.shape[1:], f32)],
    )
    return (update, moment_new, variance_new, attended)


def solution(mesh):
    fine = Mesh(mesh.devices.reshape([SIZES[name] for name in AXES]), AXES)
    fsdp = ("x", "zh", "c")
    tp = ("zl", "y")
    in_specs = (
        P(fsdp, tp),
        P(fsdp, tp),
        P(fsdp, tp),
        P(fsdp, tp),
        P(None, fsdp),
        P(None, tp),
        P(tp, fsdp),
        P(),
        P(),
        P(fsdp, None, tp),
        P(fsdp, tp, None, None),
        P(fsdp, tp, None, None),
        P(fsdp),
    )
    out_specs = (P(fsdp, tp), P(fsdp, tp), P(fsdp, tp), P(fsdp, None, tp))
    return jax.shard_map(shards, mesh=fine, in_specs=in_specs, out_specs=out_specs, check_vma=False)
```
